128 devices in a mesh: clus: 8 (over x, core), fold: 16 (over y, z).
Axes of the slice: x: 4, y: 4, z: 4, core: 2. Of those that a mesh axis runs over, the one named last changes fastest.
Arguments:
- embeddings: bfloat16 [98304, 1024], P(('clus', 'fold'))
- labels: int32 [98304], P(('clus', 'fold')), may hold values from 0 to 8, as said below
- ordinals: int32 [98304], P(('clus', 'fold')), may hold values from 0 to 12287, as said below
Outputs:
- best_match: float32 [98304], P(('clus', 'fold'))
The draws below stay inside these ranges and needn't reach their ends.
Inputs may be any that keep to these rules, and one draw needn't show every extreme that they name: `labels`: A label of 8 marks a document outside the scored clusters, whose ordinal is 0; live documents with one label have distinct ordinals. Among the 768 documents of one loader device, at most 3 live ones fall in any aligned run of 384 ordinals of one cluster, and in every cluster one loader device has exactly that many in every such run.
All inputs are finite; a program needn't handle non-finite values.
Results may differ from the reference program's by a relative error of at most 0.0003.
Values may be sent and summed in bfloat16 or wider, within the bound.
No kernel may reach another device: no remote copies, remote signals or barrier semaphores. Data moves between devices by JAX's collectives and lax.ppermute only.
A program may use at most 128 MiB of HBM per device.

```python
import jax
import jax.numpy as jnp
from jax import lax

EMB = 1024
BLK = 768
SLOT = 6
HALF = 384
CLUSTERS = 8
CAP = 12288
DOCS = 98304
N_FOLD = 16
DEVICES = 128


def routing(key):
    key = jax.random.fold_in(key, 11)
    sub_keys = jax.random.split(key, 4)
    per_half = SLOT // 2
    targets = CLUSTERS * 2 * N_FOLD
    counts = jax.random.randint(sub_keys[0], (DEVICES, targets), 0, per_half + 1)
    hot_source = jax.random.randint(sub_keys[1], (CLUSTERS,), 0, DEVICES)
    hot_target = jnp.repeat(hot_source, 2 * N_FOLD)
    cold_target = (hot_target + 1) % DEVICES
    source = jnp.arange(DEVICES, dtype=jnp.int32)[:, None]
    counts = jnp.where(source == hot_target[None, :], per_half, counts)
    counts = jnp.where(source == cold_target[None, :], 0, counts)
    slot_perm = jax.vmap(lambda one: jax.random.permutation(one, HALF))(jax.random.split(sub_keys[2], targets))
    target_ids = jnp.arange(targets, dtype=jnp.int32)
    rotation = HALF - 1 - slot_perm[target_ids, hot_target * per_half]
    slot_of = (slot_perm + rotation[:, None]) % HALF
    entry_source = jnp.arange(HALF, dtype=jnp.int32) // per_half
    entry_rank = jnp.arange(HALF, dtype=jnp.int32) % per_half
    is_live = entry_rank[None, :] < counts.T[:, entry_source]
    ordinal_of = target_ids[:, None] % (2 * N_FOLD) * HALF + slot_of
    cluster_of = jnp.broadcast_to(target_ids[:, None] // (2 * N_FOLD), (targets, HALF))
    doc_perm = jax.vmap(lambda one: jax.random.permutation(one, BLK))(jax.random.split(sub_keys[3], DEVICES))
    local_index = doc_perm[entry_source[None, :], target_ids[:, None] * per_half + entry_rank[None, :]]
    doc_index = (entry_source[None, :] * BLK + local_index).reshape(-1)
    label_values = jnp.where(is_live, cluster_of, CLUSTERS).reshape(-1).astype(jnp.int32)
    ordinal_values = jnp.where(is_live, ordinal_of, 0).reshape(-1).astype(jnp.int32)
    label_table = jnp.full((DOCS,), CLUSTERS, jnp.int32).at[doc_index].set(label_values)
    ordinal_table = jnp.zeros((DOCS,), jnp.int32).at[doc_index].set(ordinal_values)
    return (label_table, ordinal_table)


def draw_labels(key, part):
    label_table, ordinal_table = routing(key)
    return label_table


def draw_ordinals(key, part):
    label_table, ordinal_table = routing(key)
    return ordinal_table


def draw_embeddings(key, part):
    label_table, ordinal_table = routing(key)
    key = jax.random.fold_in(key, 5)
    sub_keys = jax.random.split(key, 5)
    topics = max(CAP // 4, 4)
    topic_pick = jax.random.randint(sub_keys[0], (DOCS,), 0, topics)
    centroid = jax.random.normal(sub_keys[1], (CLUSTERS + 1, EMB), jnp.float32)
    topic_table = jax.random.normal(sub_keys[2], (topics, EMB), jnp.float32)
    noise_part = jax.random.normal(sub_keys[3], (DOCS, EMB), jnp.float32)
    row_scale = jnp.exp(jax.random.uniform(sub_keys[4], (DOCS, 1), jnp.float32, -0.7, 1.4))
    rows_out = row_scale * (0.7 * centroid[label_table] + topic_table[topic_pick] + 0.7 * noise_part)
    return rows_out.astype(jnp.bfloat16)


def setup_inputs(seed: int = 0) -> dict:
    key_list = jax.random.split(jax.random.key(seed), 4)
    embeddings = draw_embeddings(jax.random.fold_in(key_list[3], 71), 0)
    labels = draw_labels(jax.random.fold_in(key_list[3], 71), 0)
    ordinals = draw_ordinals(jax.random.fold_in(key_list[3], 71), 0)
    return {"embeddings": embeddings, "labels": labels, "ordinals": ordinals}


def best_in_cluster(key_table, used_slots):

    def one_block(start):
        start = start.astype(jnp.int32)
        query_rows = lax.dynamic_slice_in_dim(key_table, start, BLK, 0)
        query_pos = start + jnp.arange(BLK, dtype=jnp.int32)

        def visit_block(step, best_sims):
            key_start = (step * BLK).astype(jnp.int32)

            def score_tile(current):
                key_rows = lax.dynamic_slice_in_dim(key_table, key_start, BLK, 0)
                key_used = lax.dynamic_slice_in_dim(used_slots, key_start, BLK, 0)
                key_pos = key_start + jnp.arange(BLK, dtype=jnp.int32)
                similarity = jnp.dot(query_rows, key_rows.T, preferred_element_type=jnp.float32)
                allowed = (key_pos[None, :] < query_pos[:, None]) & key_used[None, :]
                return jnp.maximum(current, lax.optimization_barrier(jnp.max(jnp.where(allowed, similarity, -1.0), axis=1)))
            return lax.cond(key_start <= start, score_tile, lambda current: current, best_sims)
        return lax.fori_loop(0, N_FOLD, visit_block, jnp.full((BLK,), -1.0, jnp.float32))
    return lax.map(one_block, jnp.arange(N_FOLD, dtype=jnp.int32) * BLK).reshape(CAP)

def reference(embeddings, labels, ordinals):
    widened = embeddings.astype(jnp.float32)
    square_sum = lax.optimization_barrier(jnp.sum(widened * widened, axis=1, keepdims=True)) + 1e-06
    unit_rows = (widened * lax.rsqrt(square_sum)).astype(jnp.bfloat16)
    is_live = labels < CLUSTERS
    flat_slot = jnp.where(is_live, labels * CAP + ordinals, CLUSTERS * CAP).astype(jnp.int32)
    slot_rows = jnp.zeros((CLUSTERS * CAP, EMB), jnp.bfloat16).at[flat_slot].set(unit_rows, mode='drop')
    filled = jnp.zeros((CLUSTERS * CAP,), jnp.bool_).at[flat_slot].set(True, mode='drop')
    slot_rows = slot_rows.reshape(CLUSTERS, CAP, EMB)
    filled = filled.reshape(CLUSTERS, CAP)
    results = lax.map(lambda pair: best_in_cluster(pair[0], pair[1]), (slot_rows, filled))
    table_flat = results.reshape(CLUSTERS * CAP)
    picked = table_flat[jnp.minimum(flat_slot, CLUSTERS * CAP - 1)]
    return jnp.where(is_live, picked, -1.0).astype(jnp.float32)
```

```python
import functools

import jax
import jax.numpy as jnp
from jax import lax
from jax.experimental import pallas as pl
from jax.experimental.pallas import tpu as pltpu
from jax.sharding import PartitionSpec as P

AXES = ("clus", "fold")
RING = 4
EMB = 1024
ROWS = 768
PIECES = 8
PIECE = 96
PIECE_ROWS = 112
BLOCK_ROWS = 784
HALF = 384
LANES = 128
LO = 128
FAR = 1.0e6
TILE = 256
VMEM = 48 * 1024 * 1024


def place(x, core, y, z):
    return (x % RING * 2 + core) * 16 + y % RING * 4 + z % RING


def every_device():
    for x in range(RING):
        for core in range(2):
            for y in range(RING):
                for z in range(RING):
                    yield x, core, y, z


def packet_pairs(piece):
    offset, cross = divmod(piece, 2)
    pairs = []
    for x, core, y, z in every_device():
        kind = core ^ cross
        target = place(x + offset, 0, y, z) if kind == 0 else place(x, 1, y + offset, z)
        pairs.append((place(x, core, y, z), target))
    return pairs


def block_pairs(du, dv):
    pairs = []
    for x, core, y, z in every_device():
        source = place(x, 0, y + du, z + dv) if core == 0 else place(x + du, 1, y, z - dv)
        pairs.append((source, place(x, core, y, z)))
    return pairs


def turned(pairs):
    return [(b, a) for a, b in pairs]


def whole(count):
    return [pl.BlockSpec(memory_space=pltpu.VMEM)] * count


def pack_kernel(emb_ref, labels_ref, ordinals_ref, slot_ref, *piece_refs):
    clus, fold = lax.axis_index("clus"), lax.axis_index("fold")
    core, x, y = clus % 2, clus // 2, fold // RING
    labels, ordinals = labels_ref[...], ordinals_ref[...]
    kind = labels // RING
    coordinate = jnp.where(kind == 0, x, y)
    offset = (labels % RING - coordinate + RING) % RING
    piece = 2 * offset + jnp.where(kind == core, 0, 1)
    live = labels < PIECES
    ids = lax.broadcasted_iota(jnp.int32, (16, ROWS), 0)
    member = (ids == piece) & live
    before = lax.broadcasted_iota(jnp.int32, (ROWS, ROWS), 0) < lax.broadcasted_iota(
        jnp.int32, (ROWS, ROWS), 1
    )
    counts = jnp.dot(
        jnp.where(member, 1.0, 0.0).astype(jnp.bfloat16),
        jnp.where(before, 1.0, 0.0).astype(jnp.bfloat16),
        preferred_element_type=jnp.float32,
    )
    rank = jnp.sum(jnp.where(member, counts, 0.0), axis=0, keepdims=True).astype(jnp.int32)
    slot = jnp.where(live, piece * PIECE + rank, -1)
    slot_ref[...] = slot
    chosen = lax.broadcasted_iota(jnp.int32, (ROWS, ROWS), 0) == slot
    pick = jnp.where(chosen, 1.0, 0.0).astype(jnp.bfloat16)
    high, low = ordinals // LO + 1, ordinals % LO
    row_id = lax.broadcasted_iota(jnp.int32, (16, ROWS), 0)
    codes = jnp.where(row_id == 0, high, jnp.where(row_id == 1, low, 0)).astype(jnp.float32)
    packed_codes = lax.dot_general(
        codes.astype(jnp.bfloat16),
        pick,
        (((1,), (1,)), ((), ())),
        preferred_element_type=jnp.float32,
    )
    widened = emb_ref[...].astype(jnp.float32)
    square_sum = jnp.sum(widened * widened, axis=1, keepdims=True) + 1e-6
    unit_rows = (widened * lax.rsqrt(square_sum)).astype(jnp.bfloat16)
    lane_piece = lax.broadcasted_iota(jnp.int32, (16, ROWS), 1) // PIECE
    for s in range(PIECES):
        packed = jnp.dot(
            pick[s * PIECE : (s + 1) * PIECE], unit_rows, preferred_element_type=jnp.float32
        )
        piece_refs[s][:PIECE, :] = packed.astype(jnp.bfloat16)
        mine = jnp.where(lane_piece == s, packed_codes, 0.0).astype(jnp.bfloat16)
        piece_refs[s][PIECE:, :ROWS] = mine
        piece_refs[s][PIECE:, ROWS:] = jnp.zeros((16, EMB - ROWS), jnp.bfloat16)


def join_kernel(*refs):
    piece_refs, block_ref = refs[:PIECES], refs[PIECES]
    codes = jnp.zeros((16, EMB), jnp.float32)
    for s in range(PIECES):
        block_ref[s * PIECE : (s + 1) * PIECE, :] = piece_refs[s][:PIECE, :]
        codes = codes + piece_refs[s][PIECE:, :].astype(jnp.float32)
    block_ref[ROWS:, :] = codes.astype(jnp.bfloat16)


def meet_kernel(count, steps, has_before, *refs):
    blocks, refs = refs[:count], refs[count:]
    if has_before:
        before_ref, refs = refs[0], refs[1:]
    out_ref, rows_best, lanes_best, column_ord = refs
    clus, fold = lax.axis_index("clus"), lax.axis_index("fold")
    core, x, y, z = clus % 2, clus // 2, fold // RING, fold % RING
    role = {"u": jnp.where(core == 0, y, x) // 2, "v": z // 2}
    row_ord = []
    for b in range(count):
        codes = blocks[b][ROWS:, :ROWS].astype(jnp.float32)
        high, low = codes[0:1], codes[1:2]
        line = jnp.where(high == 0.0, FAR, (high - 1.0) * LO + low)
        row_ord.append(line)
        column_ord[b] = jnp.transpose(jnp.broadcast_to(line, (LANES, ROWS)))
    rows_best[...] = jnp.full_like(rows_best, -1.0)
    lanes_best[...] = jnp.full_like(lanes_best, -1.0)
    lane_ord = out_ref

    for b in range(count):
        lane_ord[b] = jnp.broadcast_to(row_ord[b], (8, ROWS))

    def tile(a, b, a_start, b_start, a_size, b_size, both):
        a_rows, b_rows = pl.ds(a_start, a_size), pl.ds(b_start, b_size)
        scores = lax.dot_general(
            blocks[a][a_rows, :],
            blocks[b][b_rows, :],
            (((1,), (1,)), ((), ())),
            preferred_element_type=jnp.float32,
        )
        mine = column_ord[a, a_rows, :]
        theirs = lane_ord[b, 0:1, b_rows]
        best = rows_best[a, a_rows, :]
        for k in range(b_size // LANES):
            cut = slice(k * LANES, (k + 1) * LANES)
            part = scores[:, cut]
            earlier = theirs[:, cut] < mine
            best = jnp.maximum(best, jnp.where(earlier, part, -1.0))
            if both:
                later = jnp.where(earlier, -1.0, part)
                later = jnp.max(later.reshape(a_size // 8, 8, LANES), axis=0)
                if isinstance(b_start, int):
                    lanes = pl.ds(b_start + k * LANES, LANES)
                else:
                    lanes = pl.ds(pl.multiple_of(b_start + k * LANES, LANES), LANES)
                lanes_best[b, :, lanes] = jnp.maximum(lanes_best[b, :, lanes], later)
        rows_best[a, a_rows, :] = best

    for a, b, kind in steps:
        if kind in ("u", "v"):
            start = pl.multiple_of(role[kind] * HALF, HALF)
            tile(a, b, 0, HALF, HALF, HALF, True)
            tile(a, b, start, start, HALF, HALF, True)
        else:
            for i in range(0, ROWS, TILE):
                tile(a, b, i, 0, TILE, ROWS, kind is None)
    for b in range(count):
        across = jnp.transpose(rows_best[b])
        best = jnp.maximum(
            jnp.max(across, axis=0, keepdims=True),
            jnp.max(lanes_best[b], axis=0, keepdims=True),
        )
        best = jnp.broadcast_to(best, (8, ROWS))
        if has_before:
            best = jnp.maximum(best, before_ref[b])
        out_ref[b] = best


def meet(blocks, steps, before):
    count = len(blocks)
    products = sum(0.5 if kind in ("u", "v") else 1.0 for _, _, kind in steps)
    given = list(blocks) + ([] if before is None else [before])
    return pl.pallas_call(
        functools.partial(meet_kernel, count, steps, before is not None),
        out_shape=jax.ShapeDtypeStruct((count, 8, ROWS), jnp.float32),
        in_specs=whole(len(given)),
        out_specs=whole(1)[0],
        scratch_shapes=[
            pltpu.VMEM((count, ROWS, LANES), jnp.float32),
            pltpu.VMEM((count, 8, ROWS), jnp.float32),
            pltpu.VMEM((count, ROWS, LANES), jnp.float32),
        ],
        compiler_params=pltpu.CompilerParams(vmem_limit_bytes=VMEM),
        cost_estimate=pl.CostEstimate(
            flops=int(2 * products * ROWS * ROWS * EMB),
            bytes_accessed=count * BLOCK_ROWS * EMB * 2,
            transcendentals=0,
        ),
    )(*given)


def best_kernel(*refs):
    out_ref = refs[-1]
    best = refs[0][...]
    for ref in refs[1:-1]:
        best = jnp.maximum(best, ref[...])
    out_ref[...] = best


def unpack_kernel(slot_ref, *refs):
    rows, out_ref = refs[:PIECES], refs[PIECES]
    lane_piece = lax.broadcasted_iota(jnp.int32, (8, ROWS), 1) // PIECE
    line = rows[0][...]
    for s in range(1, PIECES):
        line = jnp.where(lane_piece == s, rows[s][...], line)
    column = jnp.transpose(jnp.broadcast_to(line[0:1], (LANES, ROWS)))
    slot = slot_ref[...]
    best = []
    for k in range(ROWS // LANES):
        cut = slice(k * LANES, (k + 1) * LANES)
        chosen = lax.broadcasted_iota(jnp.int32, (ROWS, LANES), 0) == slot[:, cut]
        best.append(jnp.sum(jnp.where(chosen, column, 0.0), axis=0, keepdims=True))
    found = jnp.concatenate(best, axis=1)
    out_ref[...] = jnp.where(slot >= 0, found, -1.0)


def per_device(embeddings, labels, ordinals):
    send = functools.partial(lax.ppermute, axis_name=AXES)
    slot, *pieces = pl.pallas_call(
        pack_kernel,
        out_shape=[jax.ShapeDtypeStruct((1, ROWS), jnp.int32)]
        + [jax.ShapeDtypeStruct((PIECE_ROWS, EMB), jnp.bfloat16)] * PIECES,
        in_specs=whole(3),
        out_specs=whole(1 + PIECES),
        compiler_params=pltpu.CompilerParams(vmem_limit_bytes=VMEM),
    )(embeddings, labels.reshape(1, ROWS), ordinals.reshape(1, ROWS))
    landed = [pieces[0]] + [send(pieces[s], perm=packet_pairs(s)) for s in range(1, PIECES)]
    own = pl.pallas_call(
        join_kernel,
        out_shape=jax.ShapeDtypeStruct((BLOCK_ROWS, EMB), jnp.bfloat16),
        in_specs=whole(PIECES),
        out_specs=whole(1)[0],
        compiler_params=pltpu.CompilerParams(vmem_limit_bytes=VMEM),
    )(*landed)
    up = send(own, perm=block_pairs(0, 1))
    right = send(own, perm=block_pairs(1, 0))
    left = send(own, perm=block_pairs(3, 0))
    across = send(own, perm=block_pairs(2, 0))
    up_two = send(up, perm=block_pairs(0, 1))
    first = meet([own], [(0, 0, "own")], None)
    second = meet([own, up], [(0, 1, None)], None)
    third = meet(
        [own, up, right, left],
        [(0, 2, None), (2, 3, "u"), (1, 2, None), (1, 3, None)],
        None,
    )
    fourth = meet(
        [own, up, left, across, up_two],
        [(3, 1, None), (4, 2, None), (0, 4, "v"), (3, 4, "u")],
        None,
    )
    best_own = [first[0], second[0], third[0], fourth[0]]
    back = [
        (jnp.maximum(jnp.maximum(second[1], third[1]), fourth[1]), (0, 1)),
        (third[2], (1, 0)),
        (jnp.maximum(third[3], fourth[2]), (3, 0)),
        (fourth[3], (2, 0)),
        (fourth[4], (0, 2)),
    ]
    for part, (du, dv) in back:
        best_own.append(send(part, perm=turned(block_pairs(du, dv))))
    result = best_own[0]
    for part in best_own[1:]:
        result = jnp.maximum(result, part)
    rows = [result] + [send(result, perm=turned(packet_pairs(s))) for s in range(1, PIECES)]
    scored = pl.pallas_call(
        unpack_kernel,
        out_shape=jax.ShapeDtypeStruct((1, ROWS), jnp.float32),
        in_specs=whole(1 + PIECES),
        out_specs=whole(1)[0],
        compiler_params=pltpu.CompilerParams(vmem_limit_bytes=VMEM),
    )(slot, *rows)
    return scored.reshape(ROWS)


def solution(mesh):
    return jax.shard_map(
        per_device,
        mesh=mesh,
        in_specs=(P(AXES, None), P(AXES), P(AXES)),
        out_specs=P(AXES),
        check_vma=False,
    )
```

```python
import functools

import jax
import jax.numpy as jnp
from jax import lax
from jax.experimental import pallas as pl
from jax.experimental.pallas import tpu as pltpu
from jax.sharding import PartitionSpec as P

AXES = ("clus", "fold")
RING = 4
DEVICES = 128
EMB = 1024
ROWS = 768
PIECES = 8
PIECE = 96
PIECE_ROWS = 112
HALF = 384
HALF_PIECES = 4
HALF_ROWS = 400
LANES = 128
LO = 128
FAR = 1.0e6
WIDE = 256
CHUNK = 256
VMEM = 12 * 1024 * 1024
OWN, UP, RIGHT, LEFT, OVER, UP2 = range(6)
OFFSETS = ((0, 0), (0, 1), (1, 0), (3, 0), (2, 0), (0, 2))
HALVES = 2 * len(OFFSETS)


def place(x, core, y, z):
    return (x % RING * 2 + core) * 16 + y % RING * 4 + z % RING


def every_device():
    for x in range(RING):
        for core in range(2):
            for y in range(RING):
                for z in range(RING):
                    yield x, core, y, z


def packet_pairs(piece):
    offset, cross = divmod(piece, 2)
    pairs = []
    for x, core, y, z in every_device():
        kind = core ^ cross
        target = place(x + offset, 0, y, z) if kind == 0 else place(x, 1, y + offset, z)
        pairs.append((place(x, core, y, z), target))
    return pairs


def block_pairs(du, dv):
    pairs = []
    for x, core, y, z in every_device():
        source = place(x, 0, y + du, z + dv) if core == 0 else place(x + du, 1, y, z - dv)
        pairs.append((source, place(x, core, y, z)))
    return pairs


def whole(count):
    return [pl.BlockSpec(memory_space=pltpu.VMEM)] * count


def params():
    return pltpu.CompilerParams(vmem_limit_bytes=VMEM)


def pack_kernel(emb_hbm, labels_ref, ordinals_ref, slot_ref, *refs):
    piece_refs, (emb, unit, sems) = refs[:PIECES], refs[PIECES:]
    copies = [
        pltpu.make_async_copy(
            emb_hbm.at[pl.ds(i, CHUNK)], emb.at[pl.ds(i, CHUNK)], sems.at[i // CHUNK]
        )
        for i in range(0, ROWS, CHUNK)
    ]
    for copy in copies:
        copy.start()
    clus, fold = lax.axis_index("clus"), lax.axis_index("fold")
    core, x, y = clus % 2, clus // 2, fold // RING
    labels, ordinals = labels_ref[...], ordinals_ref[...]
    kind = labels // RING
    coordinate = jnp.where(kind == 0, x, y)
    offset = (labels % RING - coordinate + RING) % RING
    piece = 2 * offset + jnp.where(kind == core, 0, 1)
    live = labels < PIECES
    ids = lax.broadcasted_iota(jnp.int32, (16, ROWS), 0)
    member = (ids == piece) & live
    before = lax.broadcasted_iota(jnp.int32, (ROWS, ROWS), 0) < lax.broadcasted_iota(
        jnp.int32, (ROWS, ROWS), 1
    )
    counts = jnp.dot(
        jnp.where(member, 1.0, 0.0).astype(jnp.bfloat16),
        jnp.where(before, 1.0, 0.0).astype(jnp.bfloat16),
        preferred_element_type=jnp.float32,
    )
    rank = jnp.sum(jnp.where(member, counts, 0.0), axis=0, keepdims=True).astype(jnp.int32)
    slot = jnp.where(live, piece * PIECE + rank, -1)
    slot_ref[...] = slot
    chosen = lax.broadcasted_iota(jnp.int32, (ROWS, ROWS), 0) == slot
    pick = jnp.where(chosen, 1.0, 0.0).astype(jnp.bfloat16)
    high, low = ordinals // LO + 1, ordinals % LO
    row_id = lax.broadcasted_iota(jnp.int32, (16, ROWS), 0)
    codes = jnp.where(row_id == 0, high, jnp.where(row_id == 1, low, 0)).astype(jnp.float32)
    packed_codes = lax.dot_general(
        codes.astype(jnp.bfloat16),
        pick,
        (((1,), (1,)), ((), ())),
        preferred_element_type=jnp.float32,
    )
    for i, copy in zip(range(0, ROWS, CHUNK), copies, strict=True):
        copy.wait()
        widened = emb[pl.ds(i, CHUNK), :].astype(jnp.float32)
        square_sum = jnp.sum(widened * widened, axis=1, keepdims=True) + 1e-6
        unit[pl.ds(i, CHUNK), :] = (widened * lax.rsqrt(square_sum)).astype(jnp.bfloat16)
    packed = jnp.dot(pick, unit[...], preferred_element_type=jnp.float32).astype(jnp.bfloat16)
    lane_piece = lax.broadcasted_iota(jnp.int32, (16, HALF), 1) // PIECE
    for s in range(PIECES):
        half, place_in_half = divmod(s, HALF_PIECES)
        piece_refs[s][:PIECE, :] = packed[s * PIECE : (s + 1) * PIECE]
        mine = packed_codes[:, half * HALF : (half + 1) * HALF]
        mine = jnp.where(lane_piece == place_in_half, mine, 0.0).astype(jnp.bfloat16)
        piece_refs[s][PIECE:, :HALF] = mine
        piece_refs[s][PIECE:, HALF:] = jnp.zeros((16, EMB - HALF), jnp.bfloat16)


def pack(embeddings, labels, ordinals):
    return pl.pallas_call(
        pack_kernel,
        out_shape=[jax.ShapeDtypeStruct((1, ROWS), jnp.int32)]
        + [jax.ShapeDtypeStruct((PIECE_ROWS, EMB), jnp.bfloat16)] * PIECES,
        in_specs=[pl.BlockSpec(memory_space=pl.ANY)] + whole(2),
        out_specs=whole(1 + PIECES),
        scratch_shapes=[
            pltpu.VMEM((ROWS, EMB), jnp.bfloat16),
            pltpu.VMEM((ROWS, EMB), jnp.bfloat16),
            pltpu.SemaphoreType.DMA((ROWS // CHUNK,)),
        ],
        compiler_params=params(),
    )(embeddings, labels.reshape(1, ROWS), ordinals.reshape(1, ROWS))


def join_kernel(*refs):
    piece_refs, half_ref = refs[:HALF_PIECES], refs[HALF_PIECES]
    codes = jnp.zeros((16, HALF), jnp.float32)
    for s in range(HALF_PIECES):
        half_ref[s * PIECE : (s + 1) * PIECE, :] = piece_refs[s][:PIECE, :]
        codes = codes + piece_refs[s][PIECE:, :HALF].astype(jnp.float32)
    half_ref[HALF:, :HALF] = codes.astype(jnp.bfloat16)
    half_ref[HALF:, HALF:] = jnp.zeros((16, EMB - HALF), jnp.bfloat16)


def join(pieces):
    return pl.pallas_call(
        join_kernel,
        out_shape=jax.ShapeDtypeStruct((HALF_ROWS, EMB), jnp.bfloat16),
        in_specs=whole(HALF_PIECES),
        out_specs=whole(1)[0],
        compiler_params=params(),
    )(*pieces)


def where_am_i():
    clus, fold = lax.axis_index("clus"), lax.axis_index("fold")
    return clus // 2, clus % 2, fold // RING, fold % RING


def post(out_ref, result_ref):
    x, core, y, z = where_am_i()
    out_ref[...] = jnp.zeros_like(out_ref)
    for slot, (du, dv) in enumerate(OFFSETS):
        for s in range(PIECES):
            half, place_in_half = divmod(s, HALF_PIECES)
            ring, cross = divmod(s, 2)
            best = jnp.max(result_ref[2 * slot + half], axis=0, keepdims=True)
            best = jnp.broadcast_to(best, (8, HALF))
            if place_in_half:
                best = pltpu.roll(best, HALF - place_in_half * PIECE, 1)
            on_zero = place(x + RING - ring, cross, y + du, z + dv)
            on_one = place(x + du, 1 - cross, y + RING - ring, z + RING - dv)
            target = jnp.where(core == 0, on_zero, on_one)
            out_ref[pl.ds(target, 1), :] = best[0:1, :LANES]


def meet_kernel(names, steps, has_before, is_last, *refs):
    blocks = dict(zip(names, refs[: len(names)], strict=True))
    refs = refs[len(names) :]
    if has_before:
        before_ref, refs = refs[0], refs[1:]
    if is_last:
        out_ref, result, rows_best, column_ord = refs
    else:
        result, rows_best, column_ord = refs
    x, core, y, z = where_am_i()
    sides = {"u": jnp.where(core == 0, y, x) // 2, "v": z // 2}

    result[...] = before_ref[...] if has_before else jnp.full_like(result, -1.0)
    lines = {}
    for name in names:
        codes = blocks[name][HALF:, :HALF].astype(jnp.float32)
        high, low = codes[0:1], codes[1:2]
        lines[name] = jnp.where(high == 0.0, FAR, (high - 1.0) * LO + low)
    firsts = list(dict.fromkeys(a for a, _, _ in steps))
    for i, name in enumerate(firsts):
        column_ord[i] = jnp.transpose(jnp.broadcast_to(lines[name], (LANES, HALF)))
        rows_best[i] = jnp.full((HALF, LANES), -1.0, jnp.float32)

    def tile(a, keys, both):
        i = firsts.index(a)
        parts = [blocks[b][start : start + size, :] for b, start, size in keys]
        scores = lax.dot_general(
            blocks[a][:HALF, :],
            parts[0] if len(parts) == 1 else jnp.concatenate(parts, axis=0),
            (((1,), (1,)), ((), ())),
            preferred_element_type=jnp.float32,
        )
        best, k = rows_best[i], 0
        for b, start, size in keys:
            for lane in range(start, start + size, LANES):
                part = scores[:, k : k + LANES]
                earlier = lines[b][:, lane : lane + LANES] < column_ord[i]
                best = jnp.maximum(best, jnp.where(earlier, part, -1.0))
                if both:
                    later = jnp.where(earlier, -1.0, part).reshape(HALF // 8, 8, LANES)
                    later = jnp.max(later, axis=0)
                    at = (2 * b[0] + b[1], slice(None), slice(lane, lane + LANES))
                    result[at] = jnp.maximum(result[at], later)
                k += LANES
        rows_best[i] = best

    def step(a, b):
        if isinstance(b, tuple):
            tile(a, [(b, 0, WIDE)], True)
            tile(a, [(b, WIDE, HALF - WIDE)], True)
        else:
            both = a[0] != b
            tile(a, [((b, 0), 0, WIDE)], both)
            tile(a, [((b, 1), 0, WIDE)], both)
            tile(a, [((b, 0), WIDE, HALF - WIDE), ((b, 1), WIDE, HALF - WIDE)], both)

    for a, b, role in steps:
        if role is None:
            step(a, b)
        else:
            pl.when(sides[role[0]] == role[1])(functools.partial(step, a, b))
    for i, name in enumerate(firsts):
        across = jnp.transpose(rows_best[i]).reshape(LANES // 8, 8, HALF)
        at = 2 * name[0] + name[1]
        result[at] = jnp.maximum(result[at], jnp.max(across, axis=0))
    if is_last:
        post(out_ref, result)


def meet(held, steps, before, is_last=False):
    names = []
    for a, b, _ in steps:
        names += [a] + ([b] if isinstance(b, tuple) else [(b, 0), (b, 1)])
    names = list(dict.fromkeys(names))
    given = [held[name] for name in names] + ([] if before is None else [before])
    products = sum(0.25 if isinstance(b, tuple) else 0.5 for _, b, _ in steps)
    firsts = len({a for a, _, _ in steps})
    best = (HALVES, 8, HALF)
    return pl.pallas_call(
        functools.partial(meet_kernel, names, steps, before is not None, is_last),
        out_shape=jax.ShapeDtypeStruct((DEVICES, LANES) if is_last else best, jnp.float32),
        in_specs=whole(len(given)),
        out_specs=whole(1)[0],
        scratch_shapes=([pltpu.VMEM(best, jnp.float32)] if is_last else [])
        + [pltpu.VMEM((firsts, HALF, LANES), jnp.float32)] * 2,
        compiler_params=params(),
        cost_estimate=pl.CostEstimate(
            flops=int(2 * products * ROWS * ROWS * EMB),
            bytes_accessed=len(names) * HALF_ROWS * EMB * 2,
            transcendentals=0,
        ),
    )(*given)


def unpack_kernel(slot_ref, got_ref, out_ref):
    x, core, y, z = where_am_i()
    slot = slot_ref[...]
    found = jnp.full((8, ROWS), -1.0, jnp.float32)
    for s in range(PIECES):
        ring, cross = divmod(s, 2)
        line = jnp.full((1, LANES), -1.0, jnp.float32)
        for du, dv in OFFSETS:
            on_zero = place(x + ring, 0, y + RING - du, z + RING - dv)
            on_one = place(x + RING - du, 1, y + ring, z + dv)
            holder = jnp.where(core == cross, on_zero, on_one)
            line = jnp.maximum(line, got_ref[pl.ds(holder, 1), :])
        column = jnp.transpose(jnp.broadcast_to(line, (LANES, LANES)))[:PIECE]
        rows = lax.broadcasted_iota(jnp.int32, (PIECE, LANES), 0) + s * PIECE
        best = []
        for k in range(0, ROWS, LANES):
            chosen = jnp.where(rows == slot[:, k : k + LANES], column, -1.0)
            best.append(jnp.max(chosen.reshape(PIECE // 8, 8, LANES), axis=0))
        found = jnp.maximum(found, jnp.concatenate(best, axis=1))
    out_ref[...] = jnp.max(found, axis=0, keepdims=True)


def unpack(slot, got):
    return pl.pallas_call(
        unpack_kernel,
        out_shape=jax.ShapeDtypeStruct((1, ROWS), jnp.float32),
        in_specs=whole(2),
        out_specs=whole(1)[0],
        compiler_params=params(),
    )(slot, got).reshape(ROWS)


def per_device(embeddings, labels, ordinals):
    send = functools.partial(lax.ppermute, axis_name=AXES)
    slot, *pieces = pack(embeddings, labels, ordinals)
    landed = [pieces[0]] + [send(pieces[s], perm=packet_pairs(s)) for s in range(1, PIECES)]
    held = {}
    for h in range(2):
        held[OWN, h] = join(landed[h * HALF_PIECES : (h + 1) * HALF_PIECES])
        held[UP, h] = send(held[OWN, h], perm=block_pairs(0, 1))
        held[RIGHT, h] = send(held[OWN, h], perm=block_pairs(1, 0))
        held[LEFT, h] = send(held[OWN, h], perm=block_pairs(3, 0))
        held[UP2, h] = send(held[UP, h], perm=block_pairs(0, 1))
    held[OVER, 0] = send(held[RIGHT, 0], perm=block_pairs(1, 0))
    held[OVER, 1] = send(held[LEFT, 1], perm=block_pairs(3, 0))
    best = meet(
        held,
        [
            ((OWN, 0), OWN, None),
            ((OWN, 1), OWN, None),
            ((UP, 0), OWN, None),
            ((RIGHT, 0), OWN, None),
            ((RIGHT, 0), (LEFT, 0), ("u", 0)),
        ],
        None,
    )
    best = meet(
        held,
        [
            ((UP, 1), OWN, None),
            ((RIGHT, 1), OWN, None),
            ((UP, 0), RIGHT, None),
            ((UP, 1), RIGHT, None),
            ((UP, 0), LEFT, None),
            ((UP, 1), LEFT, None),
            ((RIGHT, 0), (LEFT, 1), None),
            ((RIGHT, 1), (LEFT, 1), ("u", 1)),
        ],
        best,
    )
    best = meet(
        held,
        [
            ((OVER, 0), UP, None),
            ((UP2, 0), LEFT, None),
            ((UP2, 0), (OWN, 1), None),
            ((UP2, 0), (OWN, 0), ("v", 0)),
            ((UP2, 0), (OVER, 0), ("u", 0)),
        ],
        best,
    )
    best = meet(
        held,
        [((OVER, 1), UP, None), ((OVER, 1), (UP2, 0), None)],
        best,
    )
    sent = meet(
        held,
        [
            ((UP2, 1), LEFT, None),
            ((UP2, 1), (OWN, 1), ("v", 1)),
            ((UP2, 1), (OVER, 1), ("u", 1)),
        ],
        best,
        True,
    )
    got = lax.all_to_all(sent, AXES, split_axis=0, concat_axis=0, tiled=True)
    return unpack(slot, got)


def solution(mesh):
    return jax.shard_map(
        per_device,
        mesh=mesh,
        in_specs=(P(AXES, None), P(AXES), P(AXES)),
        out_specs=P(AXES),
        check_vma=False,
    )
```

```python
import functools

import jax
import jax.numpy as jnp
from jax import lax
from jax.experimental import pallas as pl
from jax.experimental.pallas import tpu as pltpu
from jax.sharding import PartitionSpec as P

AXES = ("clus", "fold")
RING = 4
DEVICES = 128
EMB = 1024
ROWS = 768
PIECES = 8
PIECE = 96
PIECE_ROWS = 112
HALF = 384
HALF_PIECES = 4
HALF_ROWS = 400
LANES = 128
LO = 128
FAR = 1.0e6
WIDE = 256
CHUNK = 256
SHOWN = 8
VMEM = 12 * 1024 * 1024
OWN, UP, RIGHT, LEFT, OVER, UP2 = range(6)
OFFSETS = ((0, 0), (0, 1), (1, 0), (3, 0), (2, 0), (0, 2))
HALVES = 2 * len(OFFSETS)


def place(x, core, y, z):
    return (x % RING * 2 + core) * 16 + y % RING * 4 + z % RING


def every_device():
    for x in range(RING):
        for core in range(2):
            for y in range(RING):
                for z in range(RING):
                    yield x, core, y, z


def packet_pairs(piece):
    offset, cross = divmod(piece, 2)
    pairs = []
    for x, core, y, z in every_device():
        kind = core ^ cross
        target = place(x + offset, 0, y, z) if kind == 0 else place(x, 1, y + offset, z)
        pairs.append((place(x, core, y, z), target))
    return pairs


def block_pairs(du, dv):
    pairs = []
    for x, core, y, z in every_device():
        source = place(x, 0, y + du, z + dv) if core == 0 else place(x + du, 1, y, z - dv)
        pairs.append((source, place(x, core, y, z)))
    return pairs


def whole(count):
    return [pl.BlockSpec(memory_space=pltpu.VMEM)] * count


def params():
    return pltpu.CompilerParams(vmem_limit_bytes=VMEM)


def pack_kernel(emb_hbm, labels_hbm, ordinals_hbm, slot_ref, *refs):
    piece_refs, (emb, labels_ref, ordinals_ref, unit, sems) = refs[:PIECES], refs[PIECES:]
    firsts = [
        pltpu.make_async_copy(labels_hbm, labels_ref, sems.at[0]),
        pltpu.make_async_copy(ordinals_hbm, ordinals_ref, sems.at[1]),
    ]
    copies = [
        pltpu.make_async_copy(
            emb_hbm.at[pl.ds(i, CHUNK)], emb.at[pl.ds(i, CHUNK)], sems.at[2 + i // CHUNK]
        )
        for i in range(0, ROWS, CHUNK)
    ]
    for copy in firsts + copies:
        copy.start()
    for copy in firsts:
        copy.wait()
    x, core, y, _ = where_am_i()
    labels = labels_ref[...].reshape(1, ROWS)
    ordinals = ordinals_ref[...].reshape(1, ROWS)
    kind = labels // RING
    coordinate = jnp.where(kind == 0, x, y)
    offset = (labels % RING - coordinate + RING) % RING
    piece = 2 * offset + jnp.where(kind == core, 0, 1)
    live = labels < PIECES
    ids = lax.broadcasted_iota(jnp.int32, (16, ROWS), 0)
    member = (ids == piece) & live
    before = lax.broadcasted_iota(jnp.int32, (ROWS, ROWS), 0) < lax.broadcasted_iota(
        jnp.int32, (ROWS, ROWS), 1
    )
    counts = jnp.dot(
        jnp.where(member, 1.0, 0.0).astype(jnp.bfloat16),
        jnp.where(before, 1.0, 0.0).astype(jnp.bfloat16),
        preferred_element_type=jnp.float32,
    )
    rank = jnp.sum(jnp.where(member, counts, 0.0), axis=0, keepdims=True).astype(jnp.int32)
    slot = jnp.where(live, piece * PIECE + rank, -1)
    slot_ref[...] = slot
    chosen = lax.broadcasted_iota(jnp.int32, (ROWS, ROWS), 0) == slot
    pick = jnp.where(chosen, 1.0, 0.0).astype(jnp.bfloat16)
    high, low = ordinals // LO + 1, ordinals % LO
    row_id = lax.broadcasted_iota(jnp.int32, (16, ROWS), 0)
    codes = jnp.where(row_id == 0, high, jnp.where(row_id == 1, low, 0)).astype(jnp.float32)
    packed_codes = lax.dot_general(
        codes.astype(jnp.bfloat16),
        pick,
        (((1,), (1,)), ((), ())),
        preferred_element_type=jnp.float32,
    )
    for i, copy in zip(range(0, ROWS, CHUNK), copies, strict=True):
        copy.wait()
        widened = emb[pl.ds(i, CHUNK), :].astype(jnp.float32)
        square_sum = jnp.sum(widened * widened, axis=1, keepdims=True) + 1e-6
        unit[pl.ds(i, CHUNK), :] = (widened * lax.rsqrt(square_sum)).astype(jnp.bfloat16)
    packed = jnp.dot(pick, unit[...], preferred_element_type=jnp.float32).astype(jnp.bfloat16)
    lane_piece = lax.broadcasted_iota(jnp.int32, (16, HALF), 1) // PIECE
    for s in range(PIECES):
        half, place_in_half = divmod(s, HALF_PIECES)
        piece_refs[s][:PIECE, :] = packed[s * PIECE : (s + 1) * PIECE]
        mine = packed_codes[:, half * HALF : (half + 1) * HALF]
        mine = jnp.where(lane_piece == place_in_half, mine, 0.0).astype(jnp.bfloat16)
        piece_refs[s][PIECE:, :HALF] = mine
        piece_refs[s][PIECE:, HALF:] = jnp.zeros((16, EMB - HALF), jnp.bfloat16)


def pack(embeddings, labels, ordinals):
    given = [pltpu.with_memory_space_constraint(v, pltpu.HBM) for v in (embeddings, labels, ordinals)]
    return pl.pallas_call(
        pack_kernel,
        out_shape=[jax.ShapeDtypeStruct((1, ROWS), jnp.int32)]
        + [jax.ShapeDtypeStruct((PIECE_ROWS, EMB), jnp.bfloat16)] * PIECES,
        in_specs=[pl.BlockSpec(memory_space=pltpu.HBM)] * 3,
        out_specs=whole(1 + PIECES),
        scratch_shapes=[
            pltpu.VMEM((ROWS, EMB), jnp.bfloat16),
            pltpu.VMEM((ROWS,), jnp.int32),
            pltpu.VMEM((ROWS,), jnp.int32),
            pltpu.VMEM((ROWS, EMB), jnp.bfloat16),
            pltpu.SemaphoreType.DMA((2 + ROWS // CHUNK,)),
        ],
        compiler_params=params(),
    )(*given)


def join_kernel(*refs):
    piece_refs, half_ref = refs[:HALF_PIECES], refs[HALF_PIECES]
    codes = jnp.zeros((16, HALF), jnp.float32)
    for s in range(HALF_PIECES):
        half_ref[s * PIECE : (s + 1) * PIECE, :] = piece_refs[s][:PIECE, :]
        codes = codes + piece_refs[s][PIECE:, :HALF].astype(jnp.float32)
    half_ref[HALF:, :HALF] = codes.astype(jnp.bfloat16)
    half_ref[HALF:, HALF:] = jnp.zeros((16, EMB - HALF), jnp.bfloat16)


def join(pieces):
    return pl.pallas_call(
        join_kernel,
        out_shape=jax.ShapeDtypeStruct((HALF_ROWS, EMB), jnp.bfloat16),
        in_specs=whole(HALF_PIECES),
        out_specs=whole(1)[0],
        compiler_params=params(),
    )(*pieces)


def where_am_i():
    clus, fold = lax.axis_index("clus"), lax.axis_index("fold")
    return clus // 2, clus % 2, fold // RING, fold % RING


def post(out_ref, result_ref):
    x, core, y, z = where_am_i()
    out_ref[...] = jnp.zeros_like(out_ref)
    for slot, (du, dv) in enumerate(OFFSETS):
        for s in range(PIECES):
            half, place_in_half = divmod(s, HALF_PIECES)
            ring, cross = divmod(s, 2)
            best = jnp.max(result_ref[2 * slot + half], axis=0, keepdims=True)
            best = jnp.broadcast_to(best, (8, HALF))
            if place_in_half:
                best = pltpu.roll(best, HALF - place_in_half * PIECE, 1)
            on_zero = place(x + RING - ring, cross, y + du, z + dv)
            on_one = place(x + du, 1 - cross, y + RING - ring, z + RING - dv)
            target = jnp.where(core == 0, on_zero, on_one)
            out_ref[pl.ds(target, 1), :] = best[0:1, :LANES]


def meet_kernel(names, steps, has_before, is_last, *refs):
    blocks = dict(zip(names, refs[: len(names)], strict=True))
    refs = refs[len(names) :]
    if has_before:
        before_ref, refs = refs[0], refs[1:]
    if is_last:
        out_ref, result, rows_best, column_ord = refs
    else:
        result, rows_best, column_ord = refs
    x, core, y, z = where_am_i()
    sides = {"u": jnp.where(core == 0, y, x) // 2, "v": z // 2}

    result[...] = before_ref[...] if has_before else jnp.full_like(result, -1.0)
    lines = {}
    for name in names:
        codes = blocks[name][HALF:, :HALF].astype(jnp.float32)
        high, low = codes[0:1], codes[1:2]
        lines[name] = jnp.where(high == 0.0, FAR, (high - 1.0) * LO + low)
    firsts = list(dict.fromkeys(a for a, _, _ in steps))
    for i, name in enumerate(firsts):
        column_ord[i] = jnp.transpose(jnp.broadcast_to(lines[name], (LANES, HALF)))
        rows_best[i] = jnp.full((HALF, LANES), -1.0, jnp.float32)

    def tile(a, keys, both):
        i = firsts.index(a)
        parts = [blocks[b][start : start + size, :] for b, start, size in keys]
        scores = lax.dot_general(
            blocks[a][:HALF, :],
            parts[0] if len(parts) == 1 else jnp.concatenate(parts, axis=0),
            (((1,), (1,)), ((), ())),
            preferred_element_type=jnp.float32,
        )
        best, k = rows_best[i], 0
        for b, start, size in keys:
            for lane in range(start, start + size, LANES):
                part = scores[:, k : k + LANES]
                earlier = lines[b][:, lane : lane + LANES] < column_ord[i]
                best = jnp.maximum(best, jnp.where(earlier, part, -1.0))
                if both:
                    later = jnp.where(earlier, -1.0, part).reshape(HALF // 8, 8, LANES)
                    later = jnp.max(later, axis=0)
                    at = (2 * b[0] + b[1], slice(None), slice(lane, lane + LANES))
                    result[at] = jnp.maximum(result[at], later)
                k += LANES
        rows_best[i] = best

    def step(a, b):
        if isinstance(b, tuple):
            tile(a, [(b, 0, WIDE)], True)
            tile(a, [(b, WIDE, HALF - WIDE)], True)
        else:
            both = a[0] != b
            tile(a, [((b, 0), 0, WIDE)], both)
            tile(a, [((b, 1), 0, WIDE)], both)
            tile(a, [((b, 0), WIDE, HALF - WIDE), ((b, 1), WIDE, HALF - WIDE)], both)

    for a, b, role in steps:
        if role is None:
            step(a, b)
        else:
            pl.when(sides[role[0]] == role[1])(functools.partial(step, a, b))
    for i, name in enumerate(firsts):
        across = jnp.transpose(rows_best[i]).reshape(LANES // 8, 8, HALF)
        at = 2 * name[0] + name[1]
        result[at] = jnp.maximum(result[at], jnp.max(across, axis=0))
    if is_last:
        post(out_ref, result)


def meet(held, steps, before, is_last=False):
    names = []
    for a, b, _ in steps:
        names += [a] + ([b] if isinstance(b, tuple) else [(b, 0), (b, 1)])
    names = list(dict.fromkeys(names))
    given = [held[name] for name in names] + ([] if before is None else [before])
    products = sum(0.25 if isinstance(b, tuple) else 0.5 for _, b, _ in steps)
    firsts = len({a for a, _, _ in steps})
    best = (HALVES, 8, HALF)
    return pl.pallas_call(
        functools.partial(meet_kernel, names, steps, before is not None, is_last),
        out_shape=jax.ShapeDtypeStruct((DEVICES, LANES) if is_last else best, jnp.float32),
        in_specs=whole(len(given)),
        out_specs=whole(1)[0],
        scratch_shapes=([pltpu.VMEM(best, jnp.float32)] if is_last else [])
        + [pltpu.VMEM((firsts, HALF, LANES), jnp.float32)] * 2,
        compiler_params=params(),
        cost_estimate=pl.CostEstimate(
            flops=int(SHOWN * products * ROWS * ROWS * EMB),
            bytes_accessed=len(names) * HALF_ROWS * EMB * 2,
            transcendentals=0,
        ),
    )(*given)


def unpack_kernel(slot_ref, got_ref, out_ref):
    x, core, y, z = where_am_i()
    slot = slot_ref[...]
    found = jnp.full((8, ROWS), -1.0, jnp.float32)
    for s in range(PIECES):
        ring, cross = divmod(s, 2)
        line = jnp.full((1, LANES), -1.0, jnp.float32)
        for du, dv in OFFSETS:
            on_zero = place(x + ring, 0, y + RING - du, z + RING - dv)
            on_one = place(x + RING - du, 1, y + ring, z + dv)
            holder = jnp.where(core == cross, on_zero, on_one)
            line = jnp.maximum(line, got_ref[pl.ds(holder, 1), :])
        column = jnp.transpose(jnp.broadcast_to(line, (LANES, LANES)))[:PIECE]
        rows = lax.broadcasted_iota(jnp.int32, (PIECE, LANES), 0) + s * PIECE
        best = []
        for k in range(0, ROWS, LANES):
            chosen = jnp.where(rows == slot[:, k : k + LANES], column, -1.0)
            best.append(jnp.max(chosen.reshape(PIECE // 8, 8, LANES), axis=0))
        found = jnp.maximum(found, jnp.concatenate(best, axis=1))
    out_ref[...] = jnp.max(found, axis=0)


def unpack(slot, got):
    return pl.pallas_call(
        unpack_kernel,
        out_shape=jax.ShapeDtypeStruct((ROWS,), jnp.float32),
        in_specs=whole(2),
        out_specs=whole(1)[0],
        compiler_params=params(),
    )(slot, got)


def per_device(embeddings, labels, ordinals):
    send = functools.partial(lax.ppermute, axis_name=AXES)
    slot, *pieces = pack(embeddings, labels, ordinals)
    landed = [pieces[0]] + [send(pieces[s], perm=packet_pairs(s)) for s in range(1, PIECES)]
    held = {}
    for h in range(2):
        held[OWN, h] = join(landed[h * HALF_PIECES : (h + 1) * HALF_PIECES])
        held[UP, h] = send(held[OWN, h], perm=block_pairs(0, 1))
        held[RIGHT, h] = send(held[OWN, h], perm=block_pairs(1, 0))
        held[LEFT, h] = send(held[OWN, h], perm=block_pairs(3, 0))
        held[UP2, h] = send(held[UP, h], perm=block_pairs(0, 1))
    held[OVER, 0] = send(held[RIGHT, 0], perm=block_pairs(1, 0))
    held[OVER, 1] = send(held[LEFT, 1], perm=block_pairs(3, 0))
    best = meet(
        held,
        [
            ((OWN, 0), OWN, None),
            ((OWN, 1), OWN, None),
            ((UP, 0), OWN, None),
            ((RIGHT, 0), OWN, None),
            ((RIGHT, 0), (LEFT, 0), ("u", 0)),
        ],
        None,
    )
    best = meet(
        held,
        [
            ((UP, 1), OWN, None),
            ((RIGHT, 1), OWN, None),
            ((UP, 0), RIGHT, None),
            ((UP, 1), RIGHT, None),
            ((UP, 0), LEFT, None),
            ((UP, 1), LEFT, None),
            ((RIGHT, 0), (LEFT, 1), None),
            ((RIGHT, 1), (LEFT, 1), ("u", 1)),
        ],
        best,
    )
    best = meet(
        held,
        [
            ((OVER, 0), UP, None),
            ((UP2, 0), LEFT, None),
            ((UP2, 0), (OWN, 1), None),
            ((UP2, 0), (OWN, 0), ("v", 0)),
            ((UP2, 0), (OVER, 0), ("u", 0)),
        ],
        best,
    )
    best = meet(
        held,
        [((OVER, 1), UP, None), ((OVER, 1), (UP2, 0), None)],
        best,
    )
    sent = meet(
        held,
        [
            ((UP2, 1), LEFT, None),
            ((UP2, 1), (OWN, 1), ("v", 1)),
            ((UP2, 1), (OVER, 1), ("u", 1)),
        ],
        best,
        True,
    )
    got = lax.all_to_all(sent, AXES, split_axis=0, concat_axis=0, tiled=True)
    return unpack(slot, got)


def solution(mesh):
    return jax.shard_map(
        per_device,
        mesh=mesh,
        in_specs=(P(AXES, None), P(AXES), P(AXES)),
        out_specs=P(AXES),
        check_vma=False,
    )
```

```python
import functools

import jax
import jax.numpy as jnp
from jax import lax
from jax.experimental import pallas as pl
from jax.experimental.pallas import tpu as pltpu
from jax.sharding import PartitionSpec as P

AXES = ("clus", "fold")
RING = 4
DEVICES = 128
EMB = 1024
ROWS = 768
PIECES = 8
PIECE = 96
HALF = 384
HALF_PIECES = 4
LANES = 128
LO = 128
FAR = 1.0e6
WIDE = 256
CHUNK = 256
VMEM = 12 * 1024 * 1024
RING_ORDER = (0, 1, 2, 3)
RING_START = tuple(2 * PIECE * RING_ORDER.index(i) for i in range(4))
SPANS = {
    "all": (0, 768),
    "top": (0, 384),
    "bottom": (384, 768),
    "near": (0, 192),
    "next": (192, 384),
    "rest": (192, 768),
}
CODE_ROWS = 16
OWN, UP, RIGHT, LEFT, OVER, UP2 = range(6)
OFFSETS = ((0, 0), (0, 1), (1, 0), (3, 0), (2, 0), (0, 2))


def place(x, core, y, z):
    return (x % RING * 2 + core) * 16 + y % RING * 4 + z % RING


def every_device():
    for x in range(RING):
        for core in range(2):
            for y in range(RING):
                for z in range(RING):
                    yield x, core, y, z


def packet_pairs(piece):
    offset, cross = divmod(piece, 2)
    pairs = []
    for x, core, y, z in every_device():
        kind = core ^ cross
        target = place(x + offset, 0, y, z) if kind == 0 else place(x, 1, y + offset, z)
        pairs.append((place(x, core, y, z), target))
    return pairs


def block_pairs(du, dv):
    pairs = []
    for x, core, y, z in every_device():
        source = place(x, 0, y + du, z + dv) if core == 0 else place(x + du, 1, y, z - dv)
        pairs.append((source, place(x, core, y, z)))
    return pairs


def whole(count):
    return [pl.BlockSpec(memory_space=pltpu.VMEM)] * count


def params():
    return pltpu.CompilerParams(vmem_limit_bytes=VMEM)


def pack_kernel(emb_hbm, labels_hbm, ordinals_hbm, slot_ref, *refs):
    piece_refs, (emb, labels_ref, ordinals_ref, unit, sems) = refs[:PIECES], refs[PIECES:]
    firsts = [
        pltpu.make_async_copy(labels_hbm, labels_ref, sems.at[0]),
        pltpu.make_async_copy(ordinals_hbm, ordinals_ref, sems.at[1]),
    ]
    copies = [
        pltpu.make_async_copy(
            emb_hbm.at[pl.ds(i, CHUNK)], emb.at[pl.ds(i, CHUNK)], sems.at[2 + i // CHUNK]
        )
        for i in range(0, ROWS, CHUNK)
    ]
    for copy in firsts + copies:
        copy.start()
    for copy in firsts:
        copy.wait()
    x, core, y, _ = where_am_i()
    labels = labels_ref[...].reshape(1, ROWS)
    ordinals = ordinals_ref[...].reshape(1, ROWS)
    kind = labels // RING
    coordinate = jnp.where(kind == 0, x, y)
    offset = (labels % RING - coordinate + RING) % RING
    cross = jnp.where(kind == core, 0, 1)
    start = jnp.zeros_like(offset)
    for ring in range(RING):
        start = jnp.where(offset == ring, RING_START[ring], start)
    live = labels < PIECES
    ids = lax.broadcasted_iota(jnp.int32, (16, ROWS), 0)
    member = (ids == 2 * offset + cross) & live
    before = lax.broadcasted_iota(jnp.int32, (ROWS, ROWS), 0) < lax.broadcasted_iota(
        jnp.int32, (ROWS, ROWS), 1
    )
    counts = jnp.dot(
        jnp.where(member, 1.0, 0.0).astype(jnp.bfloat16),
        jnp.where(before, 1.0, 0.0).astype(jnp.bfloat16),
        preferred_element_type=jnp.float32,
    )
    rank = jnp.sum(jnp.where(member, counts, 0.0), axis=0, keepdims=True).astype(jnp.int32)
    slot = jnp.where(live, start + cross * PIECE + rank, -1)
    slot_ref[...] = slot
    chosen = lax.broadcasted_iota(jnp.int32, (ROWS, ROWS), 0) == slot
    pick = jnp.where(chosen, 1.0, 0.0).astype(jnp.bfloat16)
    high, low = ordinals // LO + 1, ordinals % LO
    codes = jnp.where(ids == 0, high, jnp.where(ids == 1, low, 0)).astype(jnp.float32)
    codes = lax.dot_general(
        codes.astype(jnp.bfloat16),
        pick,
        (((1,), (1,)), ((), ())),
        preferred_element_type=jnp.float32,
    )
    for i, copy in zip(range(0, ROWS, CHUNK), copies, strict=True):
        copy.wait()
        widened = emb[pl.ds(i, CHUNK), :].astype(jnp.float32)
        square_sum = jnp.sum(widened * widened, axis=1, keepdims=True) + 1e-6
        unit[pl.ds(i, CHUNK), :] = (widened * lax.rsqrt(square_sum)).astype(jnp.bfloat16)
    packed = jnp.dot(pick, unit[...], preferred_element_type=jnp.float32).astype(jnp.bfloat16)
    lane_piece = lax.broadcasted_iota(jnp.int32, (CODE_ROWS, ROWS), 1) // PIECE
    for i, out_ref in enumerate(piece_refs):
        out_ref[:PIECE, :] = packed[i * PIECE : (i + 1) * PIECE]
        put_codes(out_ref, jnp.where(lane_piece == i, codes, 0.0))


def put_codes(ref, codes):
    ref[-CODE_ROWS:, :ROWS] = codes.astype(jnp.bfloat16)
    ref[-CODE_ROWS:, ROWS:] = jnp.zeros((CODE_ROWS, EMB - ROWS), jnp.bfloat16)


def codes_of(ref):
    return ref[-CODE_ROWS:, :ROWS].astype(jnp.float32)


def pack(embeddings, labels, ordinals):
    given = [pltpu.with_memory_space_constraint(v, pltpu.HBM) for v in (embeddings, labels, ordinals)]
    return pl.pallas_call(
        pack_kernel,
        out_shape=[jax.ShapeDtypeStruct((1, ROWS), jnp.int32)]
        + [jax.ShapeDtypeStruct((PIECE + CODE_ROWS, EMB), jnp.bfloat16)] * PIECES,
        in_specs=[pl.BlockSpec(memory_space=pltpu.HBM)] * 3,
        out_specs=whole(1 + PIECES),
        scratch_shapes=[
            pltpu.VMEM((ROWS, EMB), jnp.bfloat16),
            pltpu.VMEM((ROWS,), jnp.int32),
            pltpu.VMEM((ROWS,), jnp.int32),
            pltpu.VMEM((ROWS, EMB), jnp.bfloat16),
            pltpu.SemaphoreType.DMA((2 + ROWS // CHUNK,)),
        ],
        compiler_params=params(),
    )(*given)


def join_kernel(*refs):
    *given, out_ref = refs
    at, codes = 0, 0.0
    for ref in given:
        rows = ref.shape[0] - CODE_ROWS
        out_ref[at : at + rows, :] = ref[:rows, :]
        codes = codes + codes_of(ref)
        at += rows
    put_codes(out_ref, codes)


def join(*arrays):
    rows = sum(array.shape[0] - CODE_ROWS for array in arrays)
    return pl.pallas_call(
        join_kernel,
        out_shape=jax.ShapeDtypeStruct((rows + CODE_ROWS, EMB), jnp.bfloat16),
        in_specs=whole(len(arrays)),
        out_specs=whole(1)[0],
        compiler_params=params(),
    )(*arrays)


def close_kernel(names, steps, *refs):
    top_ref, *given = refs[: 1 + HALF_PIECES]
    bottom_ref, result, rows_best, column_ord = refs[1 + HALF_PIECES :]
    join_kernel(*given, bottom_ref)
    meet_kernel(names, steps, False, False, top_ref, bottom_ref, result, rows_best, column_ord)


def close(top, *arrays):
    names = [(OWN, "top"), (OWN, "bottom")]
    steps = [((OWN, "all"), [(OWN, "all")], None)]
    return pl.pallas_call(
        functools.partial(close_kernel, names, steps),
        out_shape=[
            jax.ShapeDtypeStruct((HALF + CODE_ROWS, EMB), jnp.bfloat16),
            jax.ShapeDtypeStruct((len(OFFSETS), 8, ROWS), jnp.float32),
        ],
        in_specs=whole(1 + HALF_PIECES),
        out_specs=whole(2),
        scratch_shapes=[pltpu.VMEM((1, ROWS, LANES), jnp.float32)] * 2,
        compiler_params=params(),
    )(top, *arrays)


def where_am_i():
    clus, fold = lax.axis_index("clus"), lax.axis_index("fold")
    return clus // 2, clus % 2, fold // RING, fold % RING


def piece_start(piece):
    return RING_START[piece // 2] + piece % 2 * PIECE


def post(out_ref, result_ref):
    x, core, y, z = where_am_i()
    out_ref[...] = jnp.zeros_like(out_ref)
    for block, (du, dv) in enumerate(OFFSETS):
        best = jnp.broadcast_to(jnp.max(result_ref[block], axis=0, keepdims=True), (8, ROWS))
        for piece in range(PIECES):
            ring, cross = divmod(piece, 2)
            start = piece_start(piece)
            mine = pltpu.roll(best, ROWS - start, 1) if start else best
            on_zero = place(x + RING - ring, cross, y + du, z + dv)
            on_one = place(x + du, 1 - cross, y + RING - ring, z + RING - dv)
            target = jnp.where(core == 0, on_zero, on_one)
            out_ref[pl.ds(target, 1), :] = mine[0:1, :LANES]


def meet_kernel(names, steps, has_before, is_last, *refs):
    parts = dict(zip(names, refs[: len(names)], strict=True))
    refs = refs[len(names) :]
    if has_before:
        before_ref, refs = refs[0], refs[1:]
    if is_last:
        out_ref, result, rows_best, column_ord = refs
    else:
        result, rows_best, column_ord = refs
    x, core, y, z = where_am_i()
    sides = {"u": jnp.where(core == 0, y, x) // 2, "v": z // 2}

    result[...] = before_ref[...] if has_before else jnp.full_like(result, -1.0)
    held = {}
    for block, part in names:
        held.setdefault(block, []).append(part)
    lines = {}
    for block, its in held.items():
        codes = sum(codes_of(parts[block, part]) for part in its)
        high, low = codes[0:1], codes[1:2]
        lines[block] = jnp.where(high == 0.0, FAR, (high - 1.0) * LO + low)
    firsts = {}
    for (block, span), _, _ in steps:
        low, high = firsts.get(block, SPANS[span])
        firsts[block] = min(low, SPANS[span][0]), max(high, SPANS[span][1])
    for i, (block, (low, high)) in enumerate(firsts.items()):
        line = jnp.broadcast_to(lines[block][:, low:high], (LANES, high - low))
        column_ord[i, low:high, :] = jnp.transpose(line)
        rows_best[i, low:high, :] = jnp.full((high - low, LANES), -1.0, jnp.float32)

    def rows_of(block, low, high):
        found = []
        for part in sorted(held[block], key=lambda p: SPANS[p]):
            start, stop = SPANS[part]
            one, two = max(low, start), min(high, stop)
            if one < two:
                found.append(parts[block, part][one - start : two - start, :])
        return found[0] if len(found) == 1 else jnp.concatenate(found, axis=0)

    def tile(a, start, stop, keys):
        i = list(firsts).index(a)
        given = [rows_of(*key) for key in keys]
        scores = lax.dot_general(
            rows_of(a, start, stop),
            given[0] if len(given) == 1 else jnp.concatenate(given, axis=0),
            (((1,), (1,)), ((), ())),
            preferred_element_type=jnp.float32,
        )
        best = rows_best[i, start:stop, :]
        ords = column_ord[i, start:stop, :]
        for k, (b, lane) in enumerate((b, n) for b, low, high in keys for n in range(low, high, LANES)):
            part = scores[:, k * LANES : (k + 1) * LANES]
            earlier = lines[b][:, lane : lane + LANES] < ords
            best = jnp.maximum(best, jnp.where(earlier, part, -1.0))
            if a != b or lane >= stop:
                later = jnp.where(earlier, -1.0, part).reshape(-1, 8, LANES)
                at = (b, slice(None), slice(lane, lane + LANES))
                result[at] = jnp.maximum(result[at], jnp.max(later, axis=0))
        rows_best[i, start:stop, :] = best

    def step(a, others):
        one, (start, stop) = a[0], SPANS[a[1]]
        lanes = [(b, n) for b, span in others for n in range(*SPANS[span], LANES)]
        tall = HALF if (stop - start) % WIDE else WIDE
        for k in range(0, len(lanes), WIDE // LANES):
            keys = []
            for b, lane in lanes[k : k + WIDE // LANES]:
                if keys and keys[-1][0] == b and keys[-1][2] == lane:
                    keys[-1] = (b, keys[-1][1], lane + LANES)
                else:
                    keys.append((b, lane, lane + LANES))
            for row in range(start, stop, tall):
                if keys[0][0] != one or keys[0][1] >= row:
                    tile(one, row, row + tall, keys)

    for a, b, role in steps:
        if role is None:
            step(a, b)
        else:
            pl.when(sides[role[0]] == role[1])(functools.partial(step, a, b))
    for i, (block, (low, high)) in enumerate(firsts.items()):
        across = jnp.transpose(rows_best[i, low:high, :]).reshape(LANES // 8, 8, high - low)
        at = (block, slice(None), slice(low, high))
        result[at] = jnp.maximum(result[at], jnp.max(across, axis=0))
    if is_last:
        post(out_ref, result)


def meet(held, steps, before, shown, is_last=False):
    names = []
    for a, b, _ in steps:
        for block, span in (a, *b):
            low, high = SPANS[span]
            names += [
                (one, part)
                for one, part in held
                if one == block and SPANS[part][0] < high and SPANS[part][1] > low
            ]
    names = list(dict.fromkeys(names))
    given = [held[name] for name in names] + ([] if before is None else [before])
    firsts = len({a[0] for a, _, _ in steps})
    best = (len(OFFSETS), 8, ROWS)
    return pl.pallas_call(
        functools.partial(meet_kernel, names, steps, before is not None, is_last),
        out_shape=jax.ShapeDtypeStruct((DEVICES, LANES) if is_last else best, jnp.float32),
        in_specs=whole(len(given)),
        out_specs=whole(1)[0],
        scratch_shapes=([pltpu.VMEM(best, jnp.float32)] if is_last else [])
        + [pltpu.VMEM((firsts, ROWS, LANES), jnp.float32)] * 2,
        compiler_params=params(),
        cost_estimate=pl.CostEstimate(
            flops=int(8 * shown * ROWS * ROWS * EMB),
            bytes_accessed=len(names) * HALF * EMB * 2,
            transcendentals=0,
        ),
    )(*given)


def unpack_kernel(slot_ref, got_ref, out_ref):
    x, core, y, z = where_am_i()
    slot = slot_ref[...]
    found = jnp.full((8, ROWS), -1.0, jnp.float32)
    for piece in range(PIECES):
        ring, cross = divmod(piece, 2)
        line = jnp.full((1, LANES), -1.0, jnp.float32)
        for du, dv in OFFSETS:
            on_zero = place(x + ring, 0, y + RING - du, z + RING - dv)
            on_one = place(x + RING - du, 1, y + ring, z + dv)
            holder = jnp.where(core == cross, on_zero, on_one)
            line = jnp.maximum(line, got_ref[pl.ds(holder, 1), :])
        column = jnp.transpose(jnp.broadcast_to(line, (LANES, LANES)))[:PIECE]
        rows = lax.broadcasted_iota(jnp.int32, (PIECE, LANES), 0) + piece_start(piece)
        best = []
        for k in range(0, ROWS, LANES):
            chosen = jnp.where(rows == slot[:, k : k + LANES], column, -1.0)
            best.append(jnp.max(chosen.reshape(PIECE // 8, 8, LANES), axis=0))
        found = jnp.maximum(found, jnp.concatenate(best, axis=1))
    out_ref[...] = jnp.max(found, axis=0)


def unpack(slot, got):
    return pl.pallas_call(
        unpack_kernel,
        out_shape=jax.ShapeDtypeStruct((ROWS,), jnp.float32),
        in_specs=whole(2),
        out_specs=whole(1)[0],
        compiler_params=params(),
    )(slot, got)


def after(array, *others):
    return lax.optimization_barrier((array, *others))[0]


def per_device(embeddings, labels, ordinals):
    send = functools.partial(lax.ppermute, axis_name=AXES)
    up, right, left = block_pairs(0, 1), block_pairs(1, 0), block_pairs(3, 0)
    slot, *pieces = pack(embeddings, labels, ordinals)
    held = {}
    landed = [pieces[0]] + [send(pieces[i], perm=packet_pairs(i)) for i in range(1, PIECES)]
    top = join(*landed[:HALF_PIECES])
    bottom, best = close(top, *landed[HALF_PIECES:])
    held[OWN, "top"], held[OWN, "bottom"] = top, bottom
    held[UP, "top"] = send(top, perm=up)
    held[UP, "bottom"] = send(bottom, perm=up)
    held[RIGHT, "top"] = send(top, perm=right)
    held[LEFT, "top"] = send(top, perm=left)
    held[RIGHT, "bottom"] = send(bottom, perm=right)
    held[LEFT, "bottom"] = send(bottom, perm=left)
    held[UP2, "top"] = send(held[UP, "top"], perm=up)
    held[UP2, "bottom"] = send(held[UP, "bottom"], perm=up)
    held[OVER, "top"] = send(held[RIGHT, "top"], perm=right)
    held[OVER, "bottom"] = send(held[LEFT, "bottom"], perm=left)
    best = meet(
        held,
        [
            ((UP, "top"), [(OWN, "all")], None),
            ((RIGHT, "top"), [(OWN, "all")], None),
            ((RIGHT, "top"), [(LEFT, "top")], ("u", 0)),
        ],
        best,
        2.25,
    )
    best = meet(
        held,
        [
            ((UP, "bottom"), [(OWN, "all")], None),
            ((RIGHT, "bottom"), [(OWN, "all")], None),
            ((UP, "all"), [(RIGHT, "all")], None),
            ((UP, "all"), [(LEFT, "all")], None),
            ((RIGHT, "top"), [(LEFT, "bottom")], None),
            ((RIGHT, "bottom"), [(LEFT, "bottom")], ("u", 1)),
        ],
        best,
        3.5,
    )
    best = meet(
        held,
        [
            ((OVER, "top"), [(UP, "all")], None),
            ((UP2, "top"), [(LEFT, "all")], None),
            ((UP2, "top"), [(OWN, "all")], ("v", 0)),
            ((UP2, "top"), [(OWN, "bottom"), (OVER, "top")], ("v", 1)),
        ],
        best,
        1.75,
    )
    best = meet(
        held, [((OVER, "bottom"), [(UP, "all"), (UP2, "top")], None)], best, 0.75
    )
    sent = meet(
        held,
        [
            ((UP2, "bottom"), [(LEFT, "all")], None),
            ((UP2, "bottom"), [(OWN, "bottom")], ("v", 1)),
            ((UP2, "bottom"), [(OVER, "bottom")], ("v", 0)),
        ],
        best,
        1.0,
        True,
    )
    got = lax.all_to_all(sent, AXES, split_axis=0, concat_axis=0, tiled=True)
    return unpack(slot, got)


def solution(mesh):
    return jax.shard_map(
        per_device,
        mesh=mesh,
        in_specs=(P(AXES, None), P(AXES), P(AXES)),
        out_specs=P(AXES),
        check_vma=False,
    )
```

```python
import functools

import jax
import jax.numpy as jnp
from jax import lax
from jax.experimental import pallas as pl
from jax.experimental.pallas import tpu as pltpu
from jax.sharding import PartitionSpec as P

AXES = ("clus", "fold")
RING = 4
DEVICES = 128
EMB = 1024
ROWS = 768
PIECES = 8
PIECE = 96
HALF = 384
HALF_PIECES = 4
LANES = 128
LO = 128
FAR = 1.0e6
WIDE = 256
CHUNK = 256
VMEM = 12 * 1024 * 1024
RING_ORDER = (0, 1, 2, 3)
RING_START = tuple(2 * PIECE * RING_ORDER.index(i) for i in range(4))
SPANS = {
    "all": (0, 768),
    "top": (0, 384),
    "bottom": (384, 768),
    "near": (0, 192),
    "next": (192, 384),
    "rest": (192, 768),
}
CODE_ROWS = 8
OWN, UP, RIGHT, LEFT, OVER, UP2 = range(6)
OFFSETS = ((0, 0), (0, 1), (1, 0), (3, 0), (2, 0), (0, 2))


def place(x, core, y, z):
    return (x % RING * 2 + core) * 16 + y % RING * 4 + z % RING


def every_device():
    for x in range(RING):
        for core in range(2):
            for y in range(RING):
                for z in range(RING):
                    yield x, core, y, z


def packet_pairs(piece):
    offset, cross = divmod(piece, 2)
    pairs = []
    for x, core, y, z in every_device():
        kind = core ^ cross
        target = place(x + offset, 0, y, z) if kind == 0 else place(x, 1, y + offset, z)
        pairs.append((place(x, core, y, z), target))
    return pairs


def block_pairs(du, dv):
    pairs = []
    for x, core, y, z in every_device():
        source = place(x, 0, y + du, z + dv) if core == 0 else place(x + du, 1, y, z - dv)
        pairs.append((source, place(x, core, y, z)))
    return pairs


def whole(count):
    return [pl.BlockSpec(memory_space=pltpu.VMEM)] * count


def params():
    return pltpu.CompilerParams(vmem_limit_bytes=VMEM)


def pack_kernel(emb_hbm, labels_hbm, ordinals_hbm, slot_ref, *refs):
    piece_refs, (emb, labels_ref, ordinals_ref, unit, sems) = refs[:PIECES], refs[PIECES:]
    firsts = [
        pltpu.make_async_copy(labels_hbm, labels_ref, sems.at[0]),
        pltpu.make_async_copy(ordinals_hbm, ordinals_ref, sems.at[1]),
    ]
    copies = [
        pltpu.make_async_copy(
            emb_hbm.at[pl.ds(i, CHUNK)], emb.at[pl.ds(i, CHUNK)], sems.at[2 + i // CHUNK]
        )
        for i in range(0, ROWS, CHUNK)
    ]
    for copy in firsts + copies:
        copy.start()
    for copy in firsts:
        copy.wait()
    x, core, y, _ = where_am_i()
    labels = labels_ref[...].reshape(1, ROWS)
    ordinals = ordinals_ref[...].reshape(1, ROWS)
    kind = labels // RING
    coordinate = jnp.where(kind == 0, x, y)
    offset = (labels % RING - coordinate + RING) % RING
    cross = jnp.where(kind == core, 0, 1)
    start = jnp.zeros_like(offset)
    for ring in range(RING):
        start = jnp.where(offset == ring, RING_START[ring], start)
    live = labels < PIECES
    ids = lax.broadcasted_iota(jnp.int32, (16, ROWS), 0)
    member = (ids == 2 * offset + cross) & live
    before = lax.broadcasted_iota(jnp.int32, (ROWS, ROWS), 0) < lax.broadcasted_iota(
        jnp.int32, (ROWS, ROWS), 1
    )
    counts = jnp.dot(
        jnp.where(member, 1.0, 0.0).astype(jnp.bfloat16),
        jnp.where(before, 1.0, 0.0).astype(jnp.bfloat16),
        preferred_element_type=jnp.float32,
    )
    rank = jnp.sum(jnp.where(member, counts, 0.0), axis=0, keepdims=True).astype(jnp.int32)
    slot = jnp.where(live, start + cross * PIECE + rank, -1)
    slot_ref[...] = slot
    chosen = lax.broadcasted_iota(jnp.int32, (ROWS, ROWS), 0) == slot
    pick = jnp.where(chosen, 1.0, 0.0).astype(jnp.bfloat16)
    high, low = ordinals // LO + 1, ordinals % LO
    codes = jnp.where(ids == 0, high, jnp.where(ids == 1, low, 0)).astype(jnp.float32)
    codes = lax.dot_general(
        codes.astype(jnp.bfloat16),
        pick,
        (((1,), (1,)), ((), ())),
        preferred_element_type=jnp.float32,
    )
    codes = codes[:CODE_ROWS]
    for i, copy in zip(range(0, ROWS, CHUNK), copies, strict=True):
        copy.wait()
        widened = emb[pl.ds(i, CHUNK), :].astype(jnp.float32)
        square_sum = jnp.sum(widened * widened, axis=1, keepdims=True) + 1e-6
        unit[pl.ds(i, CHUNK), :] = (widened * lax.rsqrt(square_sum)).astype(jnp.bfloat16)
    packed = jnp.dot(pick, unit[...], preferred_element_type=jnp.float32).astype(jnp.bfloat16)
    lane_piece = lax.broadcasted_iota(jnp.int32, (CODE_ROWS, ROWS), 1) // PIECE
    for i, out_ref in enumerate(piece_refs):
        out_ref[:PIECE, :] = packed[i * PIECE : (i + 1) * PIECE]
        put_codes(out_ref, jnp.where(lane_piece == i, codes, 0.0))


def put_codes(ref, codes):
    ref[-CODE_ROWS:, :ROWS] = codes.astype(jnp.bfloat16)
    ref[-CODE_ROWS:, ROWS:] = jnp.zeros((CODE_ROWS, EMB - ROWS), jnp.bfloat16)


def codes_of(ref):
    return ref[-CODE_ROWS:, :ROWS].astype(jnp.float32)


def pack(embeddings, labels, ordinals):
    given = [pltpu.with_memory_space_constraint(v, pltpu.HBM) for v in (embeddings, labels, ordinals)]
    return pl.pallas_call(
        pack_kernel,
        out_shape=[jax.ShapeDtypeStruct((1, ROWS), jnp.int32)]
        + [jax.ShapeDtypeStruct((PIECE + CODE_ROWS, EMB), jnp.bfloat16)] * PIECES,
        in_specs=[pl.BlockSpec(memory_space=pltpu.HBM)] * 3,
        out_specs=whole(1 + PIECES),
        scratch_shapes=[
            pltpu.VMEM((ROWS, EMB), jnp.bfloat16),
            pltpu.VMEM((ROWS,), jnp.int32),
            pltpu.VMEM((ROWS,), jnp.int32),
            pltpu.VMEM((ROWS, EMB), jnp.bfloat16),
            pltpu.SemaphoreType.DMA((2 + ROWS // CHUNK,)),
        ],
        compiler_params=params(),
    )(*given)


def join_kernel(*refs):
    *given, out_ref = refs
    at, codes = 0, 0.0
    for ref in given:
        rows = ref.shape[0] - CODE_ROWS
        out_ref[at : at + rows, :] = ref[:rows, :]
        codes = codes + codes_of(ref)
        at += rows
    put_codes(out_ref, codes)


def join(*arrays):
    rows = sum(array.shape[0] - CODE_ROWS for array in arrays)
    return pl.pallas_call(
        join_kernel,
        out_shape=jax.ShapeDtypeStruct((rows + CODE_ROWS, EMB), jnp.bfloat16),
        in_specs=whole(len(arrays)),
        out_specs=whole(1)[0],
        compiler_params=params(),
    )(*arrays)


def close_kernel(names, steps, *refs):
    top_ref, *given = refs[: 1 + HALF_PIECES]
    bottom_ref, result, rows_best, column_ord = refs[1 + HALF_PIECES :]
    join_kernel(*given, bottom_ref)
    meet_kernel(names, steps, False, False, top_ref, bottom_ref, result, rows_best, column_ord)


def close(top, *arrays):
    names = [(OWN, "top"), (OWN, "bottom")]
    steps = [((OWN, "all"), [(OWN, "all")], None)]
    return pl.pallas_call(
        functools.partial(close_kernel, names, steps),
        out_shape=[
            jax.ShapeDtypeStruct((HALF + CODE_ROWS, EMB), jnp.bfloat16),
            jax.ShapeDtypeStruct((len(OFFSETS), 8, ROWS), jnp.float32),
        ],
        in_specs=whole(1 + HALF_PIECES),
        out_specs=whole(2),
        scratch_shapes=[pltpu.VMEM((1, ROWS, LANES), jnp.float32)] * 2,
        compiler_params=params(),
    )(top, *arrays)


def where_am_i():
    clus, fold = lax.axis_index("clus"), lax.axis_index("fold")
    return clus // 2, clus % 2, fold // RING, fold % RING


def piece_start(piece):
    return RING_START[piece // 2] + piece % 2 * PIECE


def post(out_ref, result_ref):
    x, core, y, z = where_am_i()
    out_ref[...] = jnp.zeros_like(out_ref)
    for block, (du, dv) in enumerate(OFFSETS):
        best = jnp.broadcast_to(jnp.max(result_ref[block], axis=0, keepdims=True), (8, ROWS))
        for piece in range(PIECES):
            ring, cross = divmod(piece, 2)
            start = piece_start(piece)
            mine = pltpu.roll(best, ROWS - start, 1) if start else best
            on_zero = place(x + RING - ring, cross, y + du, z + dv)
            on_one = place(x + du, 1 - cross, y + RING - ring, z + RING - dv)
            target = jnp.where(core == 0, on_zero, on_one)
            out_ref[pl.ds(target, 1), :] = mine[0:1, :LANES]


def meet_kernel(names, steps, has_before, is_last, *refs):
    parts = dict(zip(names, refs[: len(names)], strict=True))
    refs = refs[len(names) :]
    if has_before:
        before_ref, refs = refs[0], refs[1:]
    if is_last:
        out_ref, result, rows_best, column_ord = refs
    else:
        result, rows_best, column_ord = refs
    x, core, y, z = where_am_i()
    sides = {"u": jnp.where(core == 0, y, x) // 2, "v": z // 2}

    result[...] = before_ref[...] if has_before else jnp.full_like(result, -1.0)
    held = {}
    for block, part in names:
        held.setdefault(block, []).append(part)
    lines = {}
    for block, its in held.items():
        codes = sum(codes_of(parts[block, part]) for part in its)
        high, low = codes[0:1], codes[1:2]
        lines[block] = jnp.where(high == 0.0, FAR, (high - 1.0) * LO + low)
    firsts = {}
    for (block, span), _, _ in steps:
        low, high = firsts.get(block, SPANS[span])
        firsts[block] = min(low, SPANS[span][0]), max(high, SPANS[span][1])
    for i, (block, (low, high)) in enumerate(firsts.items()):
        line = jnp.broadcast_to(lines[block][:, low:high], (LANES, high - low))
        column_ord[i, low:high, :] = jnp.transpose(line)
        rows_best[i, low:high, :] = jnp.full((high - low, LANES), -1.0, jnp.float32)

    def rows_of(block, low, high):
        found = []
        for part in sorted(held[block], key=lambda p: SPANS[p]):
            start, stop = SPANS[part]
            one, two = max(low, start), min(high, stop)
            if one < two:
                found.append(parts[block, part][one - start : two - start, :])
        return found[0] if len(found) == 1 else jnp.concatenate(found, axis=0)

    def tile(a, start, stop, keys):
        i = list(firsts).index(a)
        given = [rows_of(*key) for key in keys]
        scores = lax.dot_general(
            rows_of(a, start, stop),
            given[0] if len(given) == 1 else jnp.concatenate(given, axis=0),
            (((1,), (1,)), ((), ())),
            preferred_element_type=jnp.float32,
        )
        best = rows_best[i, start:stop, :]
        ords = column_ord[i, start:stop, :]
        for k, (b, lane) in enumerate((b, n) for b, low, high in keys for n in range(low, high, LANES)):
            part = scores[:, k * LANES : (k + 1) * LANES]
            earlier = lines[b][:, lane : lane + LANES] < ords
            best = jnp.maximum(best, jnp.where(earlier, part, -1.0))
            if a != b or lane >= stop:
                later = jnp.where(earlier, -1.0, part).reshape(-1, 8, LANES)
                at = (b, slice(None), slice(lane, lane + LANES))
                result[at] = jnp.maximum(result[at], jnp.max(later, axis=0))
        rows_best[i, start:stop, :] = best

    def step(a, others):
        one, (start, stop) = a[0], SPANS[a[1]]
        lanes = [(b, n) for b, span in others for n in range(*SPANS[span], LANES)]
        tall = HALF if (stop - start) % WIDE else WIDE
        for k in range(0, len(lanes), WIDE // LANES):
            keys = []
            for b, lane in lanes[k : k + WIDE // LANES]:
                if keys and keys[-1][0] == b and keys[-1][2] == lane:
                    keys[-1] = (b, keys[-1][1], lane + LANES)
                else:
                    keys.append((b, lane, lane + LANES))
            for row in range(start, stop, tall):
                if keys[0][0] != one or keys[0][1] >= row:
                    tile(one, row, row + tall, keys)

    for a, b, role in steps:
        if role is None:
            step(a, b)
        else:
            pl.when(sides[role[0]] == role[1])(functools.partial(step, a, b))
    for i, (block, (low, high)) in enumerate(firsts.items()):
        across = jnp.transpose(rows_best[i, low:high, :]).reshape(LANES // 8, 8, high - low)
        at = (block, slice(None), slice(low, high))
        result[at] = jnp.maximum(result[at], jnp.max(across, axis=0))
    if is_last:
        post(out_ref, result)


def meet(held, steps, before, shown, is_last=False):
    names = []
    for a, b, _ in steps:
        for block, span in (a, *b):
            low, high = SPANS[span]
            names += [
                (one, part)
                for one, part in held
                if one == block and SPANS[part][0] < high and SPANS[part][1] > low
            ]
    names = list(dict.fromkeys(names))
    given = [held[name] for name in names] + ([] if before is None else [before])
    firsts = len({a[0] for a, _, _ in steps})
    best = (len(OFFSETS), 8, ROWS)
    return pl.pallas_call(
        functools.partial(meet_kernel, names, steps, before is not None, is_last),
        out_shape=jax.ShapeDtypeStruct((DEVICES, LANES) if is_last else best, jnp.float32),
        in_specs=whole(len(given)),
        out_specs=whole(1)[0],
        scratch_shapes=([pltpu.VMEM(best, jnp.float32)] if is_last else [])
        + [pltpu.VMEM((firsts, ROWS, LANES), jnp.float32)] * 2,
        compiler_params=params(),
        cost_estimate=pl.CostEstimate(
            flops=int(8 * shown * ROWS * ROWS * EMB),
            bytes_accessed=len(names) * HALF * EMB * 2,
            transcendentals=0,
        ),
    )(*given)


def unpack_kernel(slot_ref, got_ref, out_ref):
    x, core, y, z = where_am_i()
    slot = slot_ref[...]
    found = jnp.full((8, ROWS), -1.0, jnp.float32)
    for piece in range(PIECES):
        ring, cross = divmod(piece, 2)
        line = jnp.full((1, LANES), -1.0, jnp.float32)
        for du, dv in OFFSETS:
            on_zero = place(x + ring, 0, y + RING - du, z + RING - dv)
            on_one = place(x + RING - du, 1, y + ring, z + dv)
            holder = jnp.where(core == cross, on_zero, on_one)
            line = jnp.maximum(line, got_ref[pl.ds(holder, 1), :])
        column = jnp.transpose(jnp.broadcast_to(line, (LANES, LANES)))[:PIECE]
        rows = lax.broadcasted_iota(jnp.int32, (PIECE, LANES), 0) + piece_start(piece)
        best = []
        for k in range(0, ROWS, LANES):
            chosen = jnp.where(rows == slot[:, k : k + LANES], column, -1.0)
            best.append(jnp.max(chosen.reshape(PIECE // 8, 8, LANES), axis=0))
        found = jnp.maximum(found, jnp.concatenate(best, axis=1))
    out_ref[...] = jnp.max(found, axis=0)


def unpack(slot, got):
    return pl.pallas_call(
        unpack_kernel,
        out_shape=jax.ShapeDtypeStruct((ROWS,), jnp.float32),
        in_specs=whole(2),
        out_specs=whole(1)[0],
        compiler_params=params(),
    )(slot, got)


def after(array, *others):
    return lax.optimization_barrier((array, *others))[0]


def per_device(embeddings, labels, ordinals):
    send = functools.partial(lax.ppermute, axis_name=AXES)
    up, right, left = block_pairs(0, 1), block_pairs(1, 0), block_pairs(3, 0)
    slot, *pieces = pack(embeddings, labels, ordinals)
    held = {}
    landed = [pieces[0]] + [send(pieces[i], perm=packet_pairs(i)) for i in range(1, PIECES)]
    top = join(*landed[:HALF_PIECES])
    bottom, best = close(top, *landed[HALF_PIECES:])
    held[OWN, "top"], held[OWN, "bottom"] = top, bottom
    held[UP, "top"] = send(top, perm=up)
    held[UP, "bottom"] = send(bottom, perm=up)
    held[RIGHT, "top"] = send(top, perm=right)
    held[LEFT, "top"] = send(top, perm=left)
    held[RIGHT, "bottom"] = send(bottom, perm=right)
    held[LEFT, "bottom"] = send(bottom, perm=left)
    held[UP2, "top"] = send(held[UP, "top"], perm=up)
    held[UP2, "bottom"] = send(held[UP, "bottom"], perm=up)
    held[OVER, "top"] = send(held[RIGHT, "top"], perm=right)
    held[OVER, "bottom"] = send(held[LEFT, "bottom"], perm=left)
    best = meet(
        held,
        [
            ((UP, "top"), [(OWN, "all")], None),
            ((RIGHT, "top"), [(OWN, "all")], None),
            ((RIGHT, "top"), [(LEFT, "top")], ("u", 0)),
        ],
        best,
        2.25,
    )
    best = meet(
        held,
        [
            ((UP, "bottom"), [(OWN, "all")], None),
            ((RIGHT, "bottom"), [(OWN, "all")], None),
            ((UP, "all"), [(RIGHT, "all")], None),
            ((UP, "all"), [(LEFT, "all")], None),
            ((RIGHT, "top"), [(LEFT, "bottom")], None),
            ((RIGHT, "bottom"), [(LEFT, "bottom")], ("u", 1)),
        ],
        best,
        3.5,
    )
    best = meet(
        held,
        [
            ((OVER, "top"), [(UP, "all")], None),
            ((UP2, "top"), [(LEFT, "all")], None),
            ((UP2, "top"), [(OWN, "all")], ("v", 0)),
            ((UP2, "top"), [(OWN, "bottom"), (OVER, "top")], ("v", 1)),
        ],
        best,
        1.75,
    )
    best = meet(
        held, [((OVER, "bottom"), [(UP, "all"), (UP2, "top")], None)], best, 0.75
    )
    sent = meet(
        held,
        [
            ((UP2, "bottom"), [(LEFT, "all")], None),
            ((UP2, "bottom"), [(OWN, "bottom")], ("v", 1)),
            ((UP2, "bottom"), [(OVER, "bottom")], ("v", 0)),
        ],
        best,
        1.0,
        True,
    )
    got = lax.all_to_all(sent, AXES, split_axis=0, concat_axis=0, tiled=True)
    return unpack(slot, got)


def solution(mesh):
    return jax.shard_map(
        per_device,
        mesh=mesh,
        in_specs=(P(AXES, None), P(AXES), P(AXES)),
        out_specs=P(AXES),
        check_vma=False,
    )
```

```python
import functools

import jax
import jax.numpy as jnp
from jax import lax
from jax.experimental import pallas as pl
from jax.experimental.pallas import tpu as pltpu
from jax.sharding import PartitionSpec as P

AXES = ("clus", "fold")
RING = 4
DEVICES = 128
EMB = 1024
ROWS = 768
PIECES = 8
PIECE = 96
HALF = 384
HALF_PIECES = 4
LANES = 128
LO = 128
FAR = 1.0e6
WIDE = 256
CHUNK = 768
VMEM = 12 * 1024 * 1024
RING_ORDER = (0, 1, 2, 3)
RING_START = tuple(2 * PIECE * RING_ORDER.index(i) for i in range(4))
SPANS = {
    "all": (0, 768),
    "top": (0, 384),
    "bottom": (384, 768),
    "near": (0, 192),
    "next": (192, 384),
    "rest": (192, 768),
}
CODE_ROWS = 8
OWN, UP, RIGHT, LEFT, OVER, UP2 = range(6)
OFFSETS = ((0, 0), (0, 1), (1, 0), (3, 0), (2, 0), (0, 2))


def place(x, core, y, z):
    return (x % RING * 2 + core) * 16 + y % RING * 4 + z % RING


def every_device():
    for x in range(RING):
        for core in range(2):
            for y in range(RING):
                for z in range(RING):
                    yield x, core, y, z


def packet_pairs(piece):
    offset, cross = divmod(piece, 2)
    pairs = []
    for x, core, y, z in every_device():
        kind = core ^ cross
        target = place(x + offset, 0, y, z) if kind == 0 else place(x, 1, y + offset, z)
        pairs.append((place(x, core, y, z), target))
    return pairs


def block_pairs(du, dv):
    pairs = []
    for x, core, y, z in every_device():
        source = place(x, 0, y + du, z + dv) if core == 0 else place(x + du, 1, y, z - dv)
        pairs.append((source, place(x, core, y, z)))
    return pairs


def whole(count):
    return [pl.BlockSpec(memory_space=pltpu.VMEM)] * count


def params():
    return pltpu.CompilerParams(vmem_limit_bytes=VMEM)


def pack_kernel(emb_hbm, labels_hbm, ordinals_hbm, slot_ref, *refs):
    piece_refs, (emb, labels_ref, ordinals_ref, unit, sems) = refs[:PIECES], refs[PIECES:]
    firsts = [
        pltpu.make_async_copy(labels_hbm, labels_ref, sems.at[0]),
        pltpu.make_async_copy(ordinals_hbm, ordinals_ref, sems.at[1]),
    ]
    copies = [
        pltpu.make_async_copy(
            emb_hbm.at[pl.ds(i, CHUNK)], emb.at[pl.ds(i, CHUNK)], sems.at[2 + i // CHUNK]
        )
        for i in range(0, ROWS, CHUNK)
    ]
    for copy in firsts + copies:
        copy.start()
    for copy in firsts:
        copy.wait()
    x, core, y, _ = where_am_i()
    labels = labels_ref[...].reshape(1, ROWS)
    ordinals = ordinals_ref[...].reshape(1, ROWS)
    kind = labels // RING
    coordinate = jnp.where(kind == 0, x, y)
    offset = (labels % RING - coordinate + RING) % RING
    cross = jnp.where(kind == core, 0, 1)
    start = jnp.zeros_like(offset)
    for ring in range(RING):
        start = jnp.where(offset == ring, RING_START[ring], start)
    live = labels < PIECES
    ids = lax.broadcasted_iota(jnp.int32, (16, ROWS), 0)
    member = (ids == 2 * offset + cross) & live
    before = lax.broadcasted_iota(jnp.int32, (ROWS, ROWS), 0) < lax.broadcasted_iota(
        jnp.int32, (ROWS, ROWS), 1
    )
    counts = jnp.dot(
        jnp.where(member, 1.0, 0.0).astype(jnp.bfloat16),
        jnp.where(before, 1.0, 0.0).astype(jnp.bfloat16),
        preferred_element_type=jnp.float32,
    )
    rank = jnp.sum(jnp.where(member, counts, 0.0), axis=0, keepdims=True).astype(jnp.int32)
    slot = jnp.where(live, start + cross * PIECE + rank, -1)
    slot_ref[...] = slot
    chosen = lax.broadcasted_iota(jnp.int32, (ROWS, ROWS), 0) == slot
    pick = jnp.where(chosen, 1.0, 0.0).astype(jnp.bfloat16)
    high, low = ordinals // LO + 1, ordinals % LO
    codes = jnp.where(ids == 0, high, jnp.where(ids == 1, low, 0)).astype(jnp.float32)
    codes = lax.dot_general(
        codes.astype(jnp.bfloat16),
        pick,
        (((1,), (1,)), ((), ())),
        preferred_element_type=jnp.float32,
    )
    codes = codes[:CODE_ROWS]
    for i, copy in zip(range(0, ROWS, CHUNK), copies, strict=True):
        copy.wait()
        widened = emb[pl.ds(i, CHUNK), :].astype(jnp.float32)
        square_sum = jnp.sum(widened * widened, axis=1, keepdims=True) + 1e-6
        unit[pl.ds(i, CHUNK), :] = (widened * lax.rsqrt(square_sum)).astype(jnp.bfloat16)
    packed = jnp.dot(pick, unit[...], preferred_element_type=jnp.float32).astype(jnp.bfloat16)
    lane_piece = lax.broadcasted_iota(jnp.int32, (CODE_ROWS, ROWS), 1) // PIECE
    for i, out_ref in enumerate(piece_refs):
        out_ref[:PIECE, :] = packed[i * PIECE : (i + 1) * PIECE]
        put_codes(out_ref, jnp.where(lane_piece == i, codes, 0.0))


def put_codes(ref, codes):
    ref[-CODE_ROWS:, :ROWS] = codes.astype(jnp.bfloat16)
    ref[-CODE_ROWS:, ROWS:] = jnp.zeros((CODE_ROWS, EMB - ROWS), jnp.bfloat16)


def codes_of(ref):
    return ref[-CODE_ROWS:, :ROWS].astype(jnp.float32)


def pack(embeddings, labels, ordinals):
    given = [pltpu.with_memory_space_constraint(v, pltpu.HBM) for v in (embeddings, labels, ordinals)]
    return pl.pallas_call(
        pack_kernel,
        out_shape=[jax.ShapeDtypeStruct((1, ROWS), jnp.int32)]
        + [jax.ShapeDtypeStruct((PIECE + CODE_ROWS, EMB), jnp.bfloat16)] * PIECES,
        in_specs=[pl.BlockSpec(memory_space=pltpu.HBM)] * 3,
        out_specs=whole(1 + PIECES),
        scratch_shapes=[
            pltpu.VMEM((ROWS, EMB), jnp.bfloat16),
            pltpu.VMEM((ROWS,), jnp.int32),
            pltpu.VMEM((ROWS,), jnp.int32),
            pltpu.VMEM((ROWS, EMB), jnp.bfloat16),
            pltpu.SemaphoreType.DMA((2 + ROWS // CHUNK,)),
        ],
        compiler_params=params(),
    )(*given)


def join_kernel(*refs):
    *given, out_ref = refs
    at, codes = 0, 0.0
    for ref in given:
        rows = ref.shape[0] - CODE_ROWS
        out_ref[at : at + rows, :] = ref[:rows, :]
        codes = codes + codes_of(ref)
        at += rows
    put_codes(out_ref, codes)


def join(*arrays):
    rows = sum(array.shape[0] - CODE_ROWS for array in arrays)
    return pl.pallas_call(
        join_kernel,
        out_shape=jax.ShapeDtypeStruct((rows + CODE_ROWS, EMB), jnp.bfloat16),
        in_specs=whole(len(arrays)),
        out_specs=whole(1)[0],
        compiler_params=params(),
    )(*arrays)


def close_kernel(names, steps, *refs):
    top_ref, *given = refs[: 1 + HALF_PIECES]
    bottom_ref, result, rows_best, column_ord = refs[1 + HALF_PIECES :]
    join_kernel(*given, bottom_ref)
    meet_kernel(names, steps, False, False, top_ref, bottom_ref, result, rows_best, column_ord)


def close(top, *arrays):
    names = [(OWN, "top"), (OWN, "bottom")]
    steps = [((OWN, "all"), [(OWN, "all")], None)]
    return pl.pallas_call(
        functools.partial(close_kernel, names, steps),
        out_shape=[
            jax.ShapeDtypeStruct((HALF + CODE_ROWS, EMB), jnp.bfloat16),
            jax.ShapeDtypeStruct((len(OFFSETS), 8, ROWS), jnp.float32),
        ],
        in_specs=whole(1 + HALF_PIECES),
        out_specs=whole(2),
        scratch_shapes=[pltpu.VMEM((1, ROWS, LANES), jnp.float32)] * 2,
        compiler_params=params(),
    )(top, *arrays)


def where_am_i():
    clus, fold = lax.axis_index("clus"), lax.axis_index("fold")
    return clus // 2, clus % 2, fold // RING, fold % RING


def piece_start(piece):
    return RING_START[piece // 2] + piece % 2 * PIECE


def post(out_ref, result_ref):
    x, core, y, z = where_am_i()
    out_ref[...] = jnp.zeros_like(out_ref)
    for block, (du, dv) in enumerate(OFFSETS):
        best = jnp.broadcast_to(jnp.max(result_ref[block], axis=0, keepdims=True), (8, ROWS))
        for piece in range(PIECES):
            ring, cross = divmod(piece, 2)
            start = piece_start(piece)
            mine = pltpu.roll(best, ROWS - start, 1) if start else best
            on_zero = place(x + RING - ring, cross, y + du, z + dv)
            on_one = place(x + du, 1 - cross, y + RING - ring, z + RING - dv)
            target = jnp.where(core == 0, on_zero, on_one)
            out_ref[pl.ds(target, 1), :] = mine[0:1, :LANES]


def meet_kernel(names, steps, has_before, is_last, *refs):
    parts = dict(zip(names, refs[: len(names)], strict=True))
    refs = refs[len(names) :]
    if has_before:
        before_ref, refs = refs[0], refs[1:]
    if is_last:
        out_ref, result, rows_best, column_ord = refs
    else:
        result, rows_best, column_ord = refs
    x, core, y, z = where_am_i()
    sides = {"u": jnp.where(core == 0, y, x) // 2, "v": z // 2}

    result[...] = before_ref[...] if has_before else jnp.full_like(result, -1.0)
    held = {}
    for block, part in names:
        held.setdefault(block, []).append(part)
    lines = {}
    for block, its in held.items():
        codes = sum(codes_of(parts[block, part]) for part in its)
        high, low = codes[0:1], codes[1:2]
        lines[block] = jnp.where(high == 0.0, FAR, (high - 1.0) * LO + low)
    firsts = {}
    for (block, span), _, _ in steps:
        low, high = firsts.get(block, SPANS[span])
        firsts[block] = min(low, SPANS[span][0]), max(high, SPANS[span][1])
    for i, (block, (low, high)) in enumerate(firsts.items()):
        line = jnp.broadcast_to(lines[block][:, low:high], (LANES, high - low))
        column_ord[i, low:high, :] = jnp.transpose(line)
        rows_best[i, low:high, :] = jnp.full((high - low, LANES), -1.0, jnp.float32)

    def rows_of(block, low, high):
        found = []
        for part in sorted(held[block], key=lambda p: SPANS[p]):
            start, stop = SPANS[part]
            one, two = max(low, start), min(high, stop)
            if one < two:
                found.append(parts[block, part][one - start : two - start, :])
        return found[0] if len(found) == 1 else jnp.concatenate(found, axis=0)

    def tile(a, start, stop, keys):
        i = list(firsts).index(a)
        given = [rows_of(*key) for key in keys]
        scores = lax.dot_general(
            rows_of(a, start, stop),
            given[0] if len(given) == 1 else jnp.concatenate(given, axis=0),
            (((1,), (1,)), ((), ())),
            preferred_element_type=jnp.float32,
        )
        best = rows_best[i, start:stop, :]
        ords = column_ord[i, start:stop, :]
        for k, (b, lane) in enumerate((b, n) for b, low, high in keys for n in range(low, high, LANES)):
            part = scores[:, k * LANES : (k + 1) * LANES]
            earlier = lines[b][:, lane : lane + LANES] < ords
            best = jnp.maximum(best, jnp.where(earlier, part, -1.0))
            if a != b or lane >= stop:
                later = jnp.where(earlier, -1.0, part).reshape(-1, 8, LANES)
                at = (b, slice(None), slice(lane, lane + LANES))
                result[at] = jnp.maximum(result[at], jnp.max(later, axis=0))
        rows_best[i, start:stop, :] = best

    def step(a, others):
        one, (start, stop) = a[0], SPANS[a[1]]
        lanes = [(b, n) for b, span in others for n in range(*SPANS[span], LANES)]
        tall = HALF if (stop - start) % WIDE else WIDE
        for k in range(0, len(lanes), WIDE // LANES):
            keys = []
            for b, lane in lanes[k : k + WIDE // LANES]:
                if keys and keys[-1][0] == b and keys[-1][2] == lane:
                    keys[-1] = (b, keys[-1][1], lane + LANES)
                else:
                    keys.append((b, lane, lane + LANES))
            for row in range(start, stop, tall):
                if keys[0][0] != one or keys[0][1] >= row:
                    tile(one, row, row + tall, keys)

    for a, b, role in steps:
        if role is None:
            step(a, b)
        else:
            pl.when(sides[role[0]] == role[1])(functools.partial(step, a, b))
    for i, (block, (low, high)) in enumerate(firsts.items()):
        across = jnp.transpose(rows_best[i, low:high, :]).reshape(LANES // 8, 8, high - low)
        at = (block, slice(None), slice(low, high))
        result[at] = jnp.maximum(result[at], jnp.max(across, axis=0))
    if is_last:
        post(out_ref, result)


def meet(held, steps, before, shown, is_last=False):
    names = []
    for a, b, _ in steps:
        for block, span in (a, *b):
            low, high = SPANS[span]
            names += [
                (one, part)
                for one, part in held
                if one == block and SPANS[part][0] < high and SPANS[part][1] > low
            ]
    names = list(dict.fromkeys(names))
    given = [held[name] for name in names] + ([] if before is None else [before])
    firsts = len({a[0] for a, _, _ in steps})
    best = (len(OFFSETS), 8, ROWS)
    return pl.pallas_call(
        functools.partial(meet_kernel, names, steps, before is not None, is_last),
        out_shape=jax.ShapeDtypeStruct((DEVICES, LANES) if is_last else best, jnp.float32),
        in_specs=whole(len(given)),
        out_specs=whole(1)[0],
        scratch_shapes=([pltpu.VMEM(best, jnp.float32)] if is_last else [])
        + [pltpu.VMEM((firsts, ROWS, LANES), jnp.float32)] * 2,
        compiler_params=params(),
        cost_estimate=pl.CostEstimate(
            flops=int(8 * shown * ROWS * ROWS * EMB),
            bytes_accessed=len(names) * HALF * EMB * 2,
            transcendentals=0,
        ),
    )(*given)


def unpack_kernel(slot_ref, got_ref, out_ref):
    x, core, y, z = where_am_i()
    slot = slot_ref[...]
    found = jnp.full((8, ROWS), -1.0, jnp.float32)
    for piece in range(PIECES):
        ring, cross = divmod(piece, 2)
        line = jnp.full((1, LANES), -1.0, jnp.float32)
        for du, dv in OFFSETS:
            on_zero = place(x + ring, 0, y + RING - du, z + RING - dv)
            on_one = place(x + RING - du, 1, y + ring, z + dv)
            holder = jnp.where(core == cross, on_zero, on_one)
            line = jnp.maximum(line, got_ref[pl.ds(holder, 1), :])
        column = jnp.transpose(jnp.broadcast_to(line, (LANES, LANES)))[:PIECE]
        rows = lax.broadcasted_iota(jnp.int32, (PIECE, LANES), 0) + piece_start(piece)
        best = []
        for k in range(0, ROWS, LANES):
            chosen = jnp.where(rows == slot[:, k : k + LANES], column, -1.0)
            best.append(jnp.max(chosen.reshape(PIECE // 8, 8, LANES), axis=0))
        found = jnp.maximum(found, jnp.concatenate(best, axis=1))
    out_ref[...] = jnp.max(found, axis=0)


def unpack(slot, got):
    return pl.pallas_call(
        unpack_kernel,
        out_shape=jax.ShapeDtypeStruct((ROWS,), jnp.float32),
        in_specs=whole(2),
        out_specs=whole(1)[0],
        compiler_params=params(),
    )(slot, got)


def after(array, *others):
    return lax.optimization_barrier((array, *others))[0]


def per_device(embeddings, labels, ordinals):
    send = functools.partial(lax.ppermute, axis_name=AXES)
    up, right, left = block_pairs(0, 1), block_pairs(1, 0), block_pairs(3, 0)
    slot, *pieces = pack(embeddings, labels, ordinals)
    held = {}
    landed = [pieces[0]] + [send(pieces[i], perm=packet_pairs(i)) for i in range(1, PIECES)]
    top = join(*landed[:HALF_PIECES])
    bottom, best = close(top, *landed[HALF_PIECES:])
    held[OWN, "top"], held[OWN, "bottom"] = top, bottom
    held[UP, "top"] = send(top, perm=up)
    held[UP, "bottom"] = send(bottom, perm=up)
    held[RIGHT, "top"] = send(top, perm=right)
    held[LEFT, "top"] = send(top, perm=left)
    held[RIGHT, "bottom"] = send(bottom, perm=right)
    held[LEFT, "bottom"] = send(bottom, perm=left)
    held[UP2, "top"] = send(held[UP, "top"], perm=up)
    held[UP2, "bottom"] = send(held[UP, "bottom"], perm=up)
    held[OVER, "top"] = send(held[RIGHT, "top"], perm=right)
    held[OVER, "bottom"] = send(held[LEFT, "bottom"], perm=left)
    best = meet(
        held,
        [
            ((UP, "top"), [(OWN, "all")], None),
            ((RIGHT, "top"), [(OWN, "all")], None),
            ((RIGHT, "top"), [(LEFT, "top")], ("u", 0)),
        ],
        best,
        2.25,
    )
    best = meet(
        held,
        [
            ((UP, "bottom"), [(OWN, "all")], None),
            ((RIGHT, "bottom"), [(OWN, "all")], None),
            ((UP, "all"), [(LEFT, "all")], None),
            ((UP, "all"), [(RIGHT, "all")], None),
            ((RIGHT, "top"), [(LEFT, "bottom")], None),
            ((RIGHT, "bottom"), [(LEFT, "bottom")], ("u", 1)),
        ],
        best,
        3.5,
    )
    best = meet(
        held,
        [
            ((OVER, "top"), [(UP, "all")], None),
            ((UP2, "top"), [(LEFT, "all")], None),
            ((UP2, "top"), [(OWN, "all")], ("v", 0)),
            ((UP2, "top"), [(OWN, "bottom"), (OVER, "top")], ("v", 1)),
        ],
        best,
        1.75,
    )
    best = meet(
        held, [((OVER, "bottom"), [(UP, "all"), (UP2, "top")], None)], best, 0.75
    )
    sent = meet(
        held,
        [
            ((UP2, "bottom"), [(LEFT, "all")], None),
            ((UP2, "bottom"), [(OWN, "bottom")], ("v", 1)),
            ((UP2, "bottom"), [(OVER, "bottom")], ("v", 0)),
        ],
        best,
        1.0,
        True,
    )
    got = lax.all_to_all(sent, AXES, split_axis=0, concat_axis=0, tiled=True)
    return unpack(slot, got)


def solution(mesh):
    return jax.shard_map(
        per_device,
        mesh=mesh,
        in_specs=(P(AXES, None), P(AXES), P(AXES)),
        out_specs=P(AXES),
        check_vma=False,
    )
```
